32 devices in a mesh: grp: 2 (over y), seq: 4 (over z), head: 2 (over x), clip: 2 (over core).
Axes of the slice: x: 2, y: 2, z: 4, core: 2. Of those that a mesh axis runs over, the one named last changes fastest.
Arguments:
- query_states: bfloat16 [4, 2048, 1536], P(('grp', 'clip'), 'seq', 'head'), parts along dimension 0, may hold values from -64 to 64
- key_states: bfloat16 [4, 2048, 1536], P(('grp', 'clip'), 'seq', 'head'), parts along dimension 0, may hold values from -4 to 4
- value_states: bfloat16 [4, 2048, 1536], P(('grp', 'clip'), 'seq', 'head'), parts along dimension 0, may hold values from -5 to 5
- output_grad: bfloat16 [4, 2048, 3072], P(('grp', 'clip'), 'seq', 'head'), parts along dimension 0, may hold values from -48 to 48
- w_out: bfloat16 [1536, 3072], P('head'), may hold values from -0.15625 to 0.15625
- key_list: int32 [4, 8, 8], P(('grp', 'clip')), parts along dimension 0, may hold values from 0 to 7, as said below
- key_count: int32 [4, 8], P(('grp', 'clip')), parts along dimension 0, may hold values from 1 to 8, as said below
Outputs:
- query_grad: bfloat16 [4, 2048, 1536], P(('grp', 'clip'), 'seq', 'head'), parts along dimension 0
- key_grad: bfloat16 [4, 2048, 1536], P(('grp', 'clip'), 'seq', 'head'), parts along dimension 0
- value_grad: bfloat16 [4, 2048, 1536], P(('grp', 'clip'), 'seq', 'head'), parts along dimension 0
- grad_features: float32 [4, 12, 3], P(('grp', 'clip'), 'head'), parts along dimension 0
The draws below stay inside these ranges and needn't reach their ends.
There are 2 independent parts, one for each index of `grp`. The reference program is written for one: setup_inputs(seed, part) draws one part's arguments, and reference() takes and returns one part's arrays. A program takes and returns all parts, laid end to end along the dimension named above; an argument that names none is the same for every part. Nothing has to cross between parts.
Inputs may be any that keep to these rules, and one draw needn't show every extreme that they name: Tile i lies in frame block i // 4 at place i % 4. For each clip and query tile i the first key_count entries of key_list are distinct key tiles in ascending order, among them i itself, each at a place within 2 of i's place, in i's frame block or in the other one; the remaining entries equal i. `key_count`: in every draw some query tile lists 8 key tiles.
All inputs are finite; a program needn't handle non-finite values.
Results may differ from the reference program's by a relative error of at most 0.035.
Values may be sent and summed in bfloat16 or wider, within the bound.
A program may use at most 128 MiB of HBM per device.

```python
import jax
import jax.numpy as jnp
from jax import lax

D = 3072
HEADS = 12
HD = 128
TILE = 256
RADIUS = 2
CLIPS = 2
TILES_DEV = 2
TILES = 8
SPATIAL = 4
TOKENS = 2048
KMAX = 8
N_SEQ = 4


def window_tables(key):
    full_clip = jax.random.randint(jax.random.fold_in(key, 11), (), 0, CLIPS)
    place_radius = jax.random.randint(jax.random.fold_in(key, 12), (CLIPS,), 1, RADIUS + 1)
    time_radius = jax.random.randint(jax.random.fold_in(key, 13), (CLIPS,), 0, 2)
    is_full = jnp.arange(CLIPS) == full_clip
    place_radius = jnp.where(is_full, RADIUS, place_radius)
    time_radius = jnp.where(is_full, 1, time_radius)
    width = min(2 * RADIUS + 1, SPATIAL)
    tile_ids = jnp.arange(TILES)
    tile_frame = tile_ids // SPATIAL
    tile_place = tile_ids % SPATIAL
    slot_ids = jnp.arange(KMAX)
    slot_frame = slot_ids // width
    slot_step = slot_ids % width
    window_start = jnp.clip(tile_place - RADIUS, 0, SPATIAL - width)
    cand_place = window_start[:, None] + slot_step[None, :]
    candidate = slot_frame[None, :] * SPATIAL + cand_place
    same_frame = slot_frame[None, :] == tile_frame[:, None]
    all_lists = []
    all_counts = []
    for clip_idx in range(CLIPS):
        near_place = jnp.abs(cand_place - tile_place[:, None]) <= place_radius[clip_idx]
        near_time = same_frame | (time_radius[clip_idx] == 1)
        valid = near_place & near_time
        order_key = jnp.where(valid, 0, KMAX) + slot_ids[None, :]
        order = jnp.argsort(order_key, axis=1, stable=True)
        sorted_cand = jnp.take_along_axis(candidate, order, axis=1)
        sorted_valid = jnp.take_along_axis(valid, order, axis=1)
        all_lists.append(jnp.where(sorted_valid, sorted_cand, tile_ids[:, None]).astype(jnp.int32))
        all_counts.append(jnp.sum(valid.astype(jnp.int32), axis=1).astype(jnp.int32))
    return (jnp.stack(all_lists), jnp.stack(all_counts))


def draw_key_list(key, part):
    return window_tables(key)[0]


def draw_key_count(key, part):
    return window_tables(key)[1]


def drawn_pair(key):
    shape = (CLIPS, TOKENS, HEADS * HD)
    keys_out = jax.random.truncated_normal(jax.random.fold_in(key, 21), -4.0, 4.0, shape, jnp.float32)
    queries = jax.random.truncated_normal(jax.random.fold_in(key, 22), -4.0, 4.0, shape, jnp.float32)
    return (queries, keys_out)


def draw_query_states(key, part):
    return drawn_pair(key)[0].astype(jnp.bfloat16)


def draw_key_states(key, part):
    return drawn_pair(key)[1].astype(jnp.bfloat16)


def draw_output_grad(key, part):
    shape = (CLIPS, TOKENS, D)
    position = jnp.arange(TOKENS).astype(jnp.float32) / TOKENS
    col_scale = jnp.exp(jax.random.uniform(jax.random.fold_in(key, 33), (D,), jnp.float32, jnp.log(0.5), jnp.log(2.0)))
    noise = jax.random.truncated_normal(jax.random.fold_in(key, 31), -4.0, 4.0, shape, jnp.float32)
    rise = jnp.exp(jnp.log(3.0) * (position - 0.5))
    row_scale = jnp.exp(jax.random.uniform(jax.random.fold_in(key, 34), (CLIPS, TOKENS), jnp.float32, jnp.log(0.3), jnp.log(3.0)))
    return (noise * (rise[None, :] * row_scale)[:, :, None] * col_scale[None, None, :]).astype(jnp.bfloat16)


def levels(key, shape, cuts, smallest, top_value):
    def one(dim, blocks):
        draws = jax.random.uniform(jax.random.fold_in(jax.random.fold_in(key, 6), dim), (blocks,), jnp.float32, smallest / len(cuts), top_value / len(cuts))
        return jnp.repeat(jnp.exp(draws), shape[dim] // blocks).reshape((-1,) + (1,) * (len(shape) - dim - 1))

    factor_of = one(*cuts[0])
    for cut in cuts[1:]:
        factor_of = factor_of * one(*cut)
    return factor_of


def scatter_about(key, extent, spread, bound, shards=(), kind=jnp.bfloat16):
    entries = spread * jax.random.normal(key, extent, jnp.float32)
    if shards:
        entries = entries * levels(key, extent, shards, -0.22, 0.18)
    return jnp.clip(entries, -bound, bound).astype(kind)


def setup_inputs(seed: int = 0, part: int = 0) -> dict:
    arg_keys = jax.random.split(jax.random.key(seed), 8)
    own_keys = jax.random.split(jax.random.fold_in(arg_keys[7], part), 8)
    query_states = draw_query_states(jax.random.fold_in(jax.random.fold_in(arg_keys[7], part), 71), part)
    key_states = draw_key_states(jax.random.fold_in(jax.random.fold_in(arg_keys[7], part), 71), part)
    value_states = scatter_about(own_keys[2], (CLIPS, TOKENS, HEADS * HD), 1.0, 5.0, ((0, 2), (1, 4), (2, 2)))
    output_grad = draw_output_grad(jax.random.fold_in(jax.random.fold_in(arg_keys[7], part), 71), part)
    w_out = scatter_about(arg_keys[4], (HEADS * HD, D), (HEADS * HD) ** -0.5, 0.15625, ((0, 2),))
    key_list = draw_key_list(jax.random.fold_in(jax.random.fold_in(arg_keys[7], part), 71), part)
    key_count = draw_key_count(jax.random.fold_in(jax.random.fold_in(arg_keys[7], part), 71), part)
    return {"query_states": query_states, "key_states": key_states, "value_states": value_states, "output_grad": output_grad, "w_out": w_out, "key_list": key_list, "key_count": key_count}


def rounded(values):
    return lax.optimization_barrier(values.astype(jnp.bfloat16)).astype(jnp.float32)


def tile_terms(query_tile, key_tiles, value_tiles, grad_tile, tile_list, tile_count):
    score_scale = HD ** -0.5
    key_rows = key_tiles[tile_list].reshape(KMAX * TILE, HEADS, HD).astype(jnp.float32)
    value_rows = value_tiles[tile_list].reshape(KMAX * TILE, HEADS, HD).astype(jnp.float32)
    query_rows = query_tile.astype(jnp.float32)
    grad_rows = grad_tile.astype(jnp.float32)
    allowed = (jnp.arange(KMAX * TILE) // TILE) < tile_count
    scores = jnp.einsum("qhe,khe->hqk", query_rows, key_rows) * score_scale
    scores = jnp.where(allowed[None, None, :], scores, -jnp.inf)
    row_max = jnp.max(scores, axis=-1, keepdims=True)
    log_norm = row_max + jnp.log(jnp.sum(jnp.exp(scores - row_max), axis=-1, keepdims=True))
    weights = jnp.exp(scores - log_norm)
    weights_b = rounded(weights)
    attn_out = rounded(jnp.einsum("hqk,khe->qhe", weights_b, value_rows))
    row_delta = jnp.sum(grad_rows * attn_out, axis=-1)
    dprob = jnp.einsum("qhe,khe->hqk", grad_rows, value_rows)
    dscore = rounded(weights * (dprob - jnp.transpose(row_delta)[:, :, None]))
    query_full = score_scale * jnp.einsum("hqk,khe->qhe", dscore, key_rows)
    key_terms = score_scale * jnp.einsum("hqk,qhe->khe", dscore, query_rows)
    value_terms = jnp.einsum("hqk,qhe->khe", weights_b, grad_rows)
    return query_full, key_terms.reshape(KMAX, TILE, HEADS, HD), value_terms.reshape(KMAX, TILE, HEADS, HD)


def clip_grads(queries, keys_in, values_in, grads, lists, counts):
    key_tiles = keys_in.reshape(TILES, TILE, HEADS, HD)
    value_tiles = values_in.reshape(TILES, TILE, HEADS, HD)
    query_blocks = queries.reshape(N_SEQ, TILES_DEV, TILE, HEADS, HD)
    grad_blocks = grads.reshape(N_SEQ, TILES_DEV, TILE, HEADS, HD)
    list_blocks = lists.reshape(N_SEQ, TILES_DEV, KMAX)
    count_blocks = counts.reshape(N_SEQ, TILES_DEV)

    def block_step(carried, inputs):
        key_acc, value_acc = carried
        query_block, grad_block, list_block, count_block = inputs
        query_full, key_terms, value_terms = jax.vmap(tile_terms, in_axes=(0, None, None, 0, 0, 0))(
            query_block, key_tiles, value_tiles, grad_block, list_block, count_block)
        live_slot = (jnp.arange(KMAX)[None, :] < count_block[:, None]).astype(jnp.float32)[:, :, None, None, None]
        flat_list = list_block.reshape(-1)
        zero_tiles = jnp.zeros((TILES, TILE, HEADS, HD), jnp.float32)
        key_part = zero_tiles.at[flat_list].add((key_terms * live_slot).reshape(-1, TILE, HEADS, HD))
        value_part = zero_tiles.at[flat_list].add((value_terms * live_slot).reshape(-1, TILE, HEADS, HD))
        return (key_acc + rounded(key_part), value_acc + rounded(value_part)), query_full

    start_acc = jnp.zeros((TILES, TILE, HEADS, HD), jnp.float32)
    (key_full, value_full), query_full = lax.scan(
        block_step, (start_acc, start_acc), (query_blocks, grad_blocks, list_blocks, count_blocks))
    return (query_full.reshape(TOKENS, HEADS, HD), key_full.reshape(TOKENS, HEADS, HD),
            value_full.reshape(TOKENS, HEADS, HD))


def reference(query_states, key_states, value_states, output_grad, w_out, key_list, key_count):
    query_outs = []
    key_outs = []
    value_outs = []
    feature_outs = []
    for clip_idx in range(CLIPS):
        grad_out = jnp.dot(output_grad[clip_idx], jnp.transpose(w_out), preferred_element_type=jnp.float32)
        grad_out = grad_out.astype(jnp.bfloat16).reshape(TOKENS, HEADS, HD)
        query_full, key_full, value_full = clip_grads(
            query_states[clip_idx].reshape(TOKENS, HEADS, HD), key_states[clip_idx].reshape(TOKENS, HEADS, HD),
            value_states[clip_idx].reshape(TOKENS, HEADS, HD), grad_out, key_list[clip_idx], key_count[clip_idx])
        features = jnp.stack([jnp.log(jnp.mean(grads_full * grads_full, axis=(0, 2)) + 1e-6)
                              for grads_full in (query_full, key_full, value_full)], axis=-1)
        query_outs.append(query_full.reshape(TOKENS, HEADS * HD).astype(jnp.bfloat16))
        key_outs.append(key_full.reshape(TOKENS, HEADS * HD).astype(jnp.bfloat16))
        value_outs.append(value_full.reshape(TOKENS, HEADS * HD).astype(jnp.bfloat16))
        feature_outs.append(features)
    return (jnp.stack(query_outs), jnp.stack(key_outs), jnp.stack(value_outs), jnp.stack(feature_outs))
```

```python
import functools
import math

import jax
import jax.numpy as jnp
from jax import lax
from jax.experimental import pallas as pl
from jax.experimental.pallas import tpu as pltpu
from jax.sharding import PartitionSpec as P

HD = 128
TILE = 256


def attend(query_tiles, key_buf, value_buf, grad_tiles, buf_slots, counts):
    score_scale = HD ** (-0.5)
    tile_count, tile_rows, feat_width = query_tiles.shape
    slot_count = buf_slots.shape[1]
    key_span = slot_count * tile_rows
    buf_tiles = key_buf.shape[0]
    key_sel = key_buf[buf_slots].reshape(tile_count, key_span, feat_width)
    value_sel = value_buf[buf_slots].reshape(tile_count, key_span, feat_width)
    allowed = jnp.arange(key_span)[None, :] // tile_rows < counts[:, None]

    def head_step(head_idx, carried):
        query_acc, key_acc, value_acc = carried
        col_start = head_idx * HD
        query_head = lax.dynamic_slice_in_dim(query_tiles, col_start, HD, 2)
        key_head = lax.dynamic_slice_in_dim(key_sel, col_start, HD, 2)
        value_head = lax.dynamic_slice_in_dim(value_sel, col_start, HD, 2)
        grad_head = lax.dynamic_slice_in_dim(grad_tiles, col_start, HD, 2)
        scores = (
            jnp.einsum("iqe,ike->iqk", query_head, key_head, preferred_element_type=jnp.float32)
            * score_scale
        )
        scores = jnp.where(allowed[:, None, :], scores, -jnp.inf)
        row_max = jnp.max(scores, axis=-1, keepdims=True)
        log_norm = row_max + jnp.log(jnp.sum(jnp.exp(scores - row_max), axis=-1, keepdims=True))
        weights = jnp.exp(scores - log_norm)
        weights_b = weights.astype(jnp.bfloat16)
        attn_out = jnp.einsum(
            "iqk,ike->iqe", weights_b, value_head, preferred_element_type=jnp.float32
        ).astype(jnp.bfloat16)
        row_delta = jnp.sum(
            grad_head.astype(jnp.float32) * attn_out.astype(jnp.float32), axis=-1, keepdims=True
        )
        dprob = jnp.einsum(
            "iqe,ike->iqk", grad_head, value_head, preferred_element_type=jnp.float32
        )
        dscore = (weights * (dprob - row_delta)).astype(jnp.bfloat16)
        query_head_grad = score_scale * jnp.einsum(
            "iqk,ike->iqe", dscore, key_head, preferred_element_type=jnp.float32
        )
        key_head_grad = score_scale * jnp.einsum(
            "iqk,iqe->ike", dscore, query_head, preferred_element_type=jnp.float32
        )
        value_head_grad = jnp.einsum(
            "iqk,iqe->ike", weights_b, grad_head, preferred_element_type=jnp.float32
        )
        query_acc = lax.dynamic_update_slice_in_dim(query_acc, query_head_grad, col_start, 2)
        key_acc = lax.dynamic_update_slice_in_dim(key_acc, key_head_grad, col_start, 2)
        value_acc = lax.dynamic_update_slice_in_dim(value_acc, value_head_grad, col_start, 2)
        return (query_acc, key_acc, value_acc)

    start_state = (
        jnp.zeros((tile_count, tile_rows, feat_width), jnp.float32),
        jnp.zeros((tile_count, key_span, feat_width), jnp.float32),
        jnp.zeros((tile_count, key_span, feat_width), jnp.float32),
    )
    query_full, key_sel_grad, value_sel_grad = lax.fori_loop(
        0, feat_width // HD, head_step, start_state
    )
    live_slot = jnp.arange(slot_count)[None, :] < counts[:, None]
    routing = (
        (buf_slots[:, :, None] == jnp.arange(buf_tiles)[None, None, :]) & live_slot[:, :, None]
    ).astype(jnp.float32)
    key_grad_buf = jnp.einsum(
        "imb,imr->br",
        routing,
        key_sel_grad.reshape(tile_count, slot_count, tile_rows * feat_width),
        precision=lax.Precision.HIGHEST,
    )
    value_grad_buf = jnp.einsum(
        "imb,imr->br",
        routing,
        value_sel_grad.reshape(tile_count, slot_count, tile_rows * feat_width),
        precision=lax.Precision.HIGHEST,
    )
    return (
        query_full,
        key_grad_buf.reshape(buf_tiles, tile_rows, feat_width),
        value_grad_buf.reshape(buf_tiles, tile_rows, feat_width),
    )


def head_squares(grads_full, head_count):
    rows = grads_full.reshape(-1, head_count, HD)
    return jnp.sum(rows * rows, axis=(0, 2))


def gathered_plan(query_states, key_states, value_states, output_grad, w_out, key_list, key_count):
    seq_count = lax.axis_size("seq")
    seq_index = lax.axis_index("seq")
    tok_rows = query_states.shape[1]
    feat_width = query_states.shape[2]
    head_count = feat_width // HD
    tile_count = tok_rows // TILE
    first_tile = seq_index * tile_count
    own_lists = lax.dynamic_slice_in_dim(key_list[0], first_tile, tile_count, 0)
    own_counts = lax.dynamic_slice_in_dim(key_count[0], first_tile, tile_count, 0)
    grad_out = lax.dot_general(
        lax.all_gather(output_grad, "head", axis=2, tiled=True)[0],
        w_out,
        (((1,), (1,)), ((), ())),
        preferred_element_type=jnp.float32,
    ).astype(jnp.bfloat16)
    query_tiles = query_states[0].reshape(tile_count, TILE, feat_width)
    grad_tiles = grad_out.reshape(tile_count, TILE, feat_width)
    key_whole, value_whole = (
        lax.all_gather(key_states, "seq", axis=1, tiled=True),
        lax.all_gather(value_states, "seq", axis=1, tiled=True),
    )
    key_buf = key_whole[0].reshape(-1, TILE, feat_width)
    value_buf = value_whole[0].reshape(-1, TILE, feat_width)
    query_full, key_grad_buf, value_grad_buf = attend(
        query_tiles, key_buf, value_buf, grad_tiles, own_lists, own_counts
    )
    buf_rows = key_grad_buf.shape[0] * TILE
    key_sum, value_sum = (
        lax.psum_scatter(
            key_grad_buf.reshape(1, buf_rows, feat_width).astype(jnp.bfloat16),
            "seq",
            scatter_dimension=1,
            tiled=True,
        ).astype(jnp.float32),
        lax.psum_scatter(
            value_grad_buf.reshape(1, buf_rows, feat_width).astype(jnp.bfloat16),
            "seq",
            scatter_dimension=1,
            tiled=True,
        ).astype(jnp.float32),
    )
    key_full = key_sum[0]
    value_full = value_sum[0]
    query_rows = query_full.reshape(tok_rows, feat_width)
    local_sums = jnp.stack(
        [
            head_squares(query_rows, head_count),
            head_squares(key_full, head_count),
            head_squares(value_full, head_count),
        ],
        axis=-1,
    )
    total_sums = lax.psum(local_sums, "seq")
    grad_features = jnp.log(total_sums / (seq_count * tok_rows * HD) + 1e-06)
    return (
        query_rows.astype(jnp.bfloat16)[None],
        key_full.astype(jnp.bfloat16)[None],
        value_full.astype(jnp.bfloat16)[None],
        grad_features[None],
    )


MESH_ID = pl.DeviceIdType.MESH
VMEM_BYTES = 58 * 1024 * 1024
NEG_BIG = -1e30
F32 = jnp.float32
BF16 = jnp.bfloat16


def dot_nt(a, b):
    return lax.dot_general(a, b, (((1,), (1,)), ((), ())), preferred_element_type=F32)


def dot_nn(a, b):
    return lax.dot_general(a, b, (((1,), (0,)), ((), ())), preferred_element_type=F32)


def fused_kernel(
    n, nh, q_ref, k_ref, v_ref, og_ref, w_ref, bias_ref,
    dq_ref, dk_ref, dv_ref, feat_ref,
    q_all, g_all, og_all, g_acc, stat_all, comb, part, chain, kt_ref, acc_k, acc_v, acc_q, sq_all,
    og_send, og_recv, q_send, q_recv, g_send, g_recv, stat_send, stat_recv,
    chain_send, chain_recv, sq_send, sq_recv,
):
    z = lax.axis_index("seq")
    hx = lax.axis_index("head")
    rows, width = q_ref.shape
    heads = width // HD
    feats = og_ref.shape[1]
    key_tiles = rows // TILE
    scale = HD ** (-0.5)
    scale2 = scale * math.log2(math.e)
    has_left = z > 0
    has_right = z < n - 1

    def remote(src, dst, ssem, rsem, axis, idx):
        return pltpu.make_async_remote_copy(
            src_ref=src, dst_ref=dst, send_sem=ssem, recv_sem=rsem,
            device_id={axis: idx}, device_id_type=MESH_ID,
        )

    def cols(h):
        return pl.ds(pl.multiple_of(h * HD, HD), HD)

    barrier = pltpu.get_barrier_semaphore()
    for i in range(1, n):
        pl.semaphore_signal(barrier, inc=1, device_id={"seq": lax.rem(z + i, n)}, device_id_type=MESH_ID)
    for i in range(1, nh):
        pl.semaphore_signal(barrier, inc=1, device_id={"head": lax.rem(hx + i, nh)}, device_id_type=MESH_ID)
    pl.semaphore_wait(barrier, n - 1 + nh - 1)

    def og_copy(i):
        return remote(og_ref, og_all.at[hx], og_send.at[i], og_recv.at[hx], "head", lax.rem(hx + i, nh))

    def og_arrival(j):
        return remote(og_all.at[j], og_all.at[j], og_send.at[0], og_recv.at[j], "head", hx)

    def q_copy(b, way):
        return remote(q_all.at[b], q_all.at[b], q_send.at[way, b], q_recv.at[b], "seq", z + (1 - 2 * way))

    def g_copy(b, h, way):
        return remote(g_all.at[b, h], g_all.at[b, h], g_send.at[way, b, h], g_recv.at[b, h], "seq", z + (1 - 2 * way))

    def stat_copy(h, i):
        return remote(stat_all.at[z, h], stat_all.at[z, h], stat_send.at[h, i], stat_recv.at[z, h], "seq", lax.rem(z + i, n))

    def stat_arrival(d, h):
        return remote(stat_all.at[d, h], stat_all.at[d, h], stat_send.at[h, 0], stat_recv.at[d, h], "seq", z)

    def chain_copy(b, h, way):
        slot = b if way == 0 else jnp.where(b == z - 1, n, b)
        return remote(part.at[b, h], chain.at[slot, h], chain_send.at[b, h], chain_recv.at[slot, h], "seq", z + (1 - 2 * way))

    def chain_arrival(slot, h):
        return remote(chain.at[slot, h], chain.at[slot, h], chain_send.at[0, h], chain_recv.at[slot, h], "seq", z)

    def sq_copy(i):
        return remote(sq_all.at[z], sq_all.at[z], sq_send.at[i], sq_recv.at[z], "seq", lax.rem(z + i, n))

    def sq_arrival(d):
        return remote(sq_all.at[d], sq_all.at[d], sq_send.at[0], sq_recv.at[d], "seq", z)

    def both_ways(copy_of):
        @pl.when(has_right)
        def _():
            copy_of(0)

        @pl.when(has_left)
        def _():
            copy_of(1)

    for i in range(1, nh):
        og_copy(i).start()
    q_all[z] = q_ref[...]
    both_ways(lambda way: q_copy(z, way).start())

    wide = 256 if width % 256 == 0 else HD

    def features_of(block, j, add):
        span = pl.ds(pl.multiple_of(j * feats, HD), feats)

        @pl.loop(0, width // wide)
        def _(c):
            at = pl.ds(pl.multiple_of(c * wide, wide), wide)
            term = dot_nt(block[...], w_ref[at, span])
            if add:
                g_acc[c] = g_acc[c] + term
            else:
                g_acc[c] = term

    features_of(og_ref, hx, False)

    def q_hop(s):
        @pl.when(z - s >= 0)
        def _():
            q_copy(z - s, 0).wait_recv()

            @pl.when(has_right)
            def _():
                q_copy(z - s, 0).start()

        @pl.when(z + s < n)
        def _():
            q_copy(z + s, 1).wait_recv()

            @pl.when(has_left)
            def _():
                q_copy(z + s, 1).start()

    early = min(2, n - 1)
    for s in range(1, early + 1):
        q_hop(s)
    for i in range(1, nh):
        j = lax.rem(hx + i, nh)
        og_arrival(j).wait_recv()
        features_of(og_all.at[j], j, True)
    for h in range(heads):
        lo = h * HD
        g_all[z, h] = g_acc[lo // wide, :, lo % wide : lo % wide + HD].astype(BF16)
        both_ways(lambda way: g_copy(z, h, way).start())
    for s in range(early + 1, n):
        q_hop(s)

    def g_hop(s, h):
        @pl.when((h >= 0) & (h < heads))
        def _():
            @pl.when(z - s >= 0)
            def _():
                g_copy(z - s, h, 0).wait_recv()
                if s < n - 1:
                    @pl.when(has_right)
                    def _():
                        g_copy(z - s, h, 0).start()

            @pl.when(z + s < n)
            def _():
                g_copy(z + s, h, 1).wait_recv()
                if s < n - 1:
                    @pl.when(has_left)
                    def _():
                        g_copy(z + s, h, 1).start()

    def logits(b, h, j):
        t = dot_nt(k_ref[j * TILE : (j + 1) * TILE, cols(h)], q_all[b, :, cols(h)])
        return t * scale2 + bias_ref[b, j : j + 1, :]

    def dprobs(b, h, j):
        return dot_nt(v_ref[j * TILE : (j + 1) * TILE, cols(h)], g_all[b, h])

    def first_pass(h):
        @pl.loop(0, n)
        def _(b):
            ts = [logits(b, h, j) for j in range(key_tiles)]
            top = functools.reduce(jnp.maximum, [jnp.max(t, axis=0, keepdims=True) for t in ts])
            total = jnp.zeros((1, rows), F32)
            eps = jnp.zeros((1, rows), F32)
            for j in range(key_tiles):
                p = jnp.exp2(ts[j] - top)
                total += jnp.sum(p, axis=0, keepdims=True)
                eps += jnp.sum(p * dprobs(b, h, j), axis=0, keepdims=True)
            stat_all[z, h, b, 0:1, :] = top + jnp.log2(total)
            stat_all[z, h, b, 1:2, :] = eps / total

        for i in range(1, n):
            stat_copy(h, i).start()

    def second_pass(h):
        for i in range(1, n):
            stat_arrival(lax.rem(z + i, n), h).wait_recv()
        for b in range(n):
            logs = [stat_all[d, h, b, 0:1, :] for d in range(n)]
            top = functools.reduce(jnp.maximum, logs)
            log_norm = top + jnp.log2(sum(jnp.exp2(x - top) for x in logs))
            comb[b, 0:1, :] = log_norm
            comb[b, 1:2, :] = sum(
                jnp.exp2(logs[d] - log_norm) * stat_all[d, h, b, 1:2, :] for d in range(n)
            )
        kt_ref[...] = jnp.transpose(k_ref[:, cols(h)].astype(F32)).astype(BF16)
        acc_k[...] = jnp.zeros_like(acc_k)
        acc_v[...] = jnp.zeros_like(acc_v)

        @pl.loop(0, n)
        def _(b):
            q_b = q_all[b, :, cols(h)]
            g_b = g_all[b, h]
            dq_t = jnp.zeros((HD, rows), F32)
            for j in range(key_tiles):
                at = slice(j * TILE, (j + 1) * TILE)
                p = jnp.exp2(logits(b, h, j) - comb[b, 0:1, :])
                ds = (p * (dprobs(b, h, j) - comb[b, 1:2, :])).astype(BF16)
                acc_v[at, :] += dot_nn(p.astype(BF16), g_b)
                acc_k[at, :] += dot_nn(ds, q_b)
                dq_t += dot_nn(kt_ref[:, at], ds)
            part[b, h] = (dq_t * scale).astype(BF16)

        key_full = acc_k[...] * scale
        value_full = acc_v[...]
        dk_ref[:, cols(h)] = key_full.astype(BF16)
        dv_ref[:, cols(h)] = value_full.astype(BF16)
        sq_all[z, 1, h] = jnp.sum(key_full * key_full, axis=0, keepdims=True)
        sq_all[z, 2, h] = jnp.sum(value_full * value_full, axis=0, keepdims=True)

    def chain_hop(h, way):
        first = has_left if way == 0 else has_right

        @pl.when((h >= 0) & (h < heads))
        def _():
            for i in range(1, n):
                b = z + i if way == 0 else z - i

                @pl.when((b >= 0) & (b < n))
                def _():
                    @pl.when(first)
                    def _():
                        chain_arrival(b, h).wait_recv()
                        part[b, h] = (part[b, h].astype(F32) + chain[b, h].astype(F32)).astype(BF16)

                    chain_copy(b, h, way).start()

    def own_sum(h):
        @pl.when((h >= 0) & (h < heads))
        def _():
            acc_q[...] = part[z, h].astype(F32)

            @pl.when(has_left)
            def _():
                chain_arrival(z, h).wait_recv()
                acc_q[...] += chain[z, h].astype(F32)

            @pl.when(has_right)
            def _():
                chain_arrival(n, h).wait_recv()
                acc_q[...] += chain[n, h].astype(F32)

            query_full = jnp.transpose(acc_q[...])
            dq_ref[:, cols(h)] = query_full.astype(BF16)
            sq_all[z, 0, h] = jnp.sum(query_full * query_full, axis=0, keepdims=True)

    lead = max(n - 2, 0)

    @pl.loop(0, lead + heads + n)
    def _(step):
        t = step - lead
        for s in range(1, n):
            g_hop(s, t + (n - 1 - s))

        @pl.when((t >= 0) & (t < heads))
        def _():
            first_pass(t)

        @pl.when((t >= 1) & (t <= heads))
        def _():
            second_pass(t - 1)

        chain_hop(t - 1 - z, 0)
        chain_hop(t - 1 - (n - 1 - z), 1)
        own_sum(t - 1 - jnp.maximum(z, n - 1 - z))

    for i in range(1, n):
        sq_copy(i).start()
    for i in range(1, n):
        sq_arrival(lax.rem(z + i, n)).wait_recv()
    total = functools.reduce(jnp.add, [sq_all[d] for d in range(n)])
    mean = jnp.sum(total, axis=-1, keepdims=True) / (n * rows * HD)
    feat_ref[...] = jnp.broadcast_to(jnp.log(mean + 1e-06), feat_ref.shape)

    for i in range(1, nh):
        og_copy(i).wait_send()
    for i in range(1, n):
        sq_copy(i).wait_send()
    both_ways(lambda way: q_copy(z, way).wait_send())
    for s in range(1, n - 1):
        @pl.when((z - s >= 0) & has_right)
        def _():
            q_copy(z - s, 0).wait_send()

        @pl.when((z + s < n) & has_left)
        def _():
            q_copy(z + s, 1).wait_send()

    @pl.loop(0, heads)
    def _(h):
        both_ways(lambda way: g_copy(z, h, way).wait_send())
        for s in range(1, n - 1):
            @pl.when((z - s >= 0) & has_right)
            def _():
                g_copy(z - s, h, 0).wait_send()

            @pl.when((z + s < n) & has_left)
            def _():
                g_copy(z + s, h, 1).wait_send()
        for i in range(1, n):
            stat_copy(h, i).wait_send()

            @pl.when(z + i < n)
            def _():
                chain_copy(z + i, h, 0).wait_send()

            @pl.when(z - i >= 0)
            def _():
                chain_copy(z - i, h, 1).wait_send()


def fused_bytes(n, nh, rows, width, feats):
    block = rows * width * 2
    return block * (6 + 3 * n + n + 1) + rows * feats * 2 * (1 + nh) + width * feats * nh * 2 + 2 * block


def per_device(query_states, key_states, value_states, output_grad, w_out, key_list, key_count):
    n = lax.axis_size("seq")
    nh = lax.axis_size("head")
    rows, width = query_states.shape[1:]
    feats = output_grad.shape[2]
    if n < 2 or fused_bytes(n, nh, rows, width, feats) > VMEM_BYTES * 3 // 4:
        return gathered_plan(
            query_states, key_states, value_states, output_grad, w_out, key_list, key_count
        )
    heads = width // HD
    key_tiles = rows // TILE
    tiles, slots = key_list.shape[1:]
    own_tiles = lax.axis_index("seq") * key_tiles + jnp.arange(key_tiles)
    live = jnp.arange(slots)[None, :] < key_count[0][:, None]
    listed = (key_list[0][:, :, None] == own_tiles[None, None, :]) & live[:, :, None]
    bias = jnp.where(jnp.any(listed, axis=1), 0.0, NEG_BIG).astype(F32)
    bias = jnp.repeat(bias.reshape(n, key_tiles, key_tiles), TILE, axis=1).transpose(0, 2, 1)
    wide = 256 if width % 256 == 0 else HD
    vmem = pl.BlockSpec(memory_space=pltpu.VMEM)
    dma = pltpu.SemaphoreType.DMA
    block = jax.ShapeDtypeStruct((rows, width), BF16)
    dq, dk, dv, feat = pl.pallas_call(
        functools.partial(fused_kernel, n, nh),
        out_shape=[block, block, block, jax.ShapeDtypeStruct((3, heads, 1, HD), F32)],
        in_specs=[vmem] * 6,
        out_specs=[vmem] * 4,
        scratch_shapes=[
            pltpu.VMEM((n, rows, width), BF16),
            pltpu.VMEM((n, heads, rows, HD), BF16),
            pltpu.VMEM((nh, rows, feats), BF16),
            pltpu.VMEM((width // wide, rows, wide), F32),
            pltpu.VMEM((n, heads, n, 2, rows), F32),
            pltpu.VMEM((n, 2, rows), F32),
            pltpu.VMEM((n, heads, HD, rows), BF16),
            pltpu.VMEM((n + 1, heads, HD, rows), BF16),
            pltpu.VMEM((HD, rows), BF16),
            pltpu.VMEM((rows, HD), F32),
            pltpu.VMEM((rows, HD), F32),
            pltpu.VMEM((HD, rows), F32),
            pltpu.VMEM((n, 3, heads, 1, HD), F32),
            dma((nh,)), dma((nh,)),
            dma((2, n)), dma((n,)),
            dma((2, n, heads)), dma((n, heads)),
            dma((heads, n)), dma((n, heads)),
            dma((n, heads)), dma((n + 1, heads)),
            dma((n,)), dma((n,)),
        ],
        compiler_params=pltpu.CompilerParams(
            collective_id=0, has_side_effects=True, vmem_limit_bytes=VMEM_BYTES
        ),
        cost_estimate=pl.CostEstimate(
            flops=14 * rows * rows * n * width + 2 * rows * width * feats * nh,
            bytes_accessed=16 * rows * width,
            transcendentals=2 * rows * rows * n * heads,
        ),
    )(query_states[0], key_states[0], value_states[0], output_grad[0], w_out, bias)
    grad_features = jnp.transpose(feat[:, :, 0, 0])
    return dq[None], dk[None], dv[None], grad_features[None]


def solution(mesh):
    in_specs = (
        P(("grp", "clip"), "seq", "head"),
        P(("grp", "clip"), "seq", "head"),
        P(("grp", "clip"), "seq", "head"),
        P(("grp", "clip"), "seq", "head"),
        P("head", None),
        P(("grp", "clip"), None, None),
        P(("grp", "clip"), None),
    )
    out_specs = (
        P(("grp", "clip"), "seq", "head"),
        P(("grp", "clip"), "seq", "head"),
        P(("grp", "clip"), "seq", "head"),
        P(("grp", "clip"), "head", None),
    )
    return jax.shard_map(
        per_device, mesh=mesh, in_specs=in_specs, out_specs=out_specs, check_vma=False
    )
```

```python
import functools
import math

import jax
import jax.numpy as jnp
from jax import lax
from jax.experimental import pallas as pl
from jax.experimental.pallas import tpu as pltpu
from jax.sharding import PartitionSpec as P

HD = 128
TILE = 256


def attend(query_tiles, key_buf, value_buf, grad_tiles, buf_slots, counts):
    score_scale = HD ** (-0.5)
    tile_count, tile_rows, feat_width = query_tiles.shape
    slot_count = buf_slots.shape[1]
    key_span = slot_count * tile_rows
    buf_tiles = key_buf.shape[0]
    key_sel = key_buf[buf_slots].reshape(tile_count, key_span, feat_width)
    value_sel = value_buf[buf_slots].reshape(tile_count, key_span, feat_width)
    allowed = jnp.arange(key_span)[None, :] // tile_rows < counts[:, None]

    def head_step(head_idx, carried):
        query_acc, key_acc, value_acc = carried
        col_start = head_idx * HD
        query_head = lax.dynamic_slice_in_dim(query_tiles, col_start, HD, 2)
        key_head = lax.dynamic_slice_in_dim(key_sel, col_start, HD, 2)
        value_head = lax.dynamic_slice_in_dim(value_sel, col_start, HD, 2)
        grad_head = lax.dynamic_slice_in_dim(grad_tiles, col_start, HD, 2)
        scores = (
            jnp.einsum("iqe,ike->iqk", query_head, key_head, preferred_element_type=jnp.float32)
            * score_scale
        )
        scores = jnp.where(allowed[:, None, :], scores, -jnp.inf)
        row_max = jnp.max(scores, axis=-1, keepdims=True)
        log_norm = row_max + jnp.log(jnp.sum(jnp.exp(scores - row_max), axis=-1, keepdims=True))
        weights = jnp.exp(scores - log_norm)
        weights_b = weights.astype(jnp.bfloat16)
        attn_out = jnp.einsum(
            "iqk,ike->iqe", weights_b, value_head, preferred_element_type=jnp.float32
        ).astype(jnp.bfloat16)
        row_delta = jnp.sum(
            grad_head.astype(jnp.float32) * attn_out.astype(jnp.float32), axis=-1, keepdims=True
        )
        dprob = jnp.einsum(
            "iqe,ike->iqk", grad_head, value_head, preferred_element_type=jnp.float32
        )
        dscore = (weights * (dprob - row_delta)).astype(jnp.bfloat16)
        query_head_grad = score_scale * jnp.einsum(
            "iqk,ike->iqe", dscore, key_head, preferred_element_type=jnp.float32
        )
        key_head_grad = score_scale * jnp.einsum(
            "iqk,iqe->ike", dscore, query_head, preferred_element_type=jnp.float32
        )
        value_head_grad = jnp.einsum(
            "iqk,iqe->ike", weights_b, grad_head, preferred_element_type=jnp.float32
        )
        query_acc = lax.dynamic_update_slice_in_dim(query_acc, query_head_grad, col_start, 2)
        key_acc = lax.dynamic_update_slice_in_dim(key_acc, key_head_grad, col_start, 2)
        value_acc = lax.dynamic_update_slice_in_dim(value_acc, value_head_grad, col_start, 2)
        return (query_acc, key_acc, value_acc)

    start_state = (
        jnp.zeros((tile_count, tile_rows, feat_width), jnp.float32),
        jnp.zeros((tile_count, key_span, feat_width), jnp.float32),
        jnp.zeros((tile_count, key_span, feat_width), jnp.float32),
    )
    query_full, key_sel_grad, value_sel_grad = lax.fori_loop(
        0, feat_width // HD, head_step, start_state
    )
    live_slot = jnp.arange(slot_count)[None, :] < counts[:, None]
    routing = (
        (buf_slots[:, :, None] == jnp.arange(buf_tiles)[None, None, :]) & live_slot[:, :, None]
    ).astype(jnp.float32)
    key_grad_buf = jnp.einsum(
        "imb,imr->br",
        routing,
        key_sel_grad.reshape(tile_count, slot_count, tile_rows * feat_width),
        precision=lax.Precision.HIGHEST,
    )
    value_grad_buf = jnp.einsum(
        "imb,imr->br",
        routing,
        value_sel_grad.reshape(tile_count, slot_count, tile_rows * feat_width),
        precision=lax.Precision.HIGHEST,
    )
    return (
        query_full,
        key_grad_buf.reshape(buf_tiles, tile_rows, feat_width),
        value_grad_buf.reshape(buf_tiles, tile_rows, feat_width),
    )


def head_squares(grads_full, head_count):
    rows = grads_full.reshape(-1, head_count, HD)
    return jnp.sum(rows * rows, axis=(0, 2))


def gathered_plan(query_states, key_states, value_states, output_grad, w_out, key_list, key_count):
    seq_count = lax.axis_size("seq")
    seq_index = lax.axis_index("seq")
    tok_rows = query_states.shape[1]
    feat_width = query_states.shape[2]
    head_count = feat_width // HD
    tile_count = tok_rows // TILE
    first_tile = seq_index * tile_count
    own_lists = lax.dynamic_slice_in_dim(key_list[0], first_tile, tile_count, 0)
    own_counts = lax.dynamic_slice_in_dim(key_count[0], first_tile, tile_count, 0)
    grad_out = lax.dot_general(
        lax.all_gather(output_grad, "head", axis=2, tiled=True)[0],
        w_out,
        (((1,), (1,)), ((), ())),
        preferred_element_type=jnp.float32,
    ).astype(jnp.bfloat16)
    query_tiles = query_states[0].reshape(tile_count, TILE, feat_width)
    grad_tiles = grad_out.reshape(tile_count, TILE, feat_width)
    key_whole, value_whole = (
        lax.all_gather(key_states, "seq", axis=1, tiled=True),
        lax.all_gather(value_states, "seq", axis=1, tiled=True),
    )
    key_buf = key_whole[0].reshape(-1, TILE, feat_width)
    value_buf = value_whole[0].reshape(-1, TILE, feat_width)
    query_full, key_grad_buf, value_grad_buf = attend(
        query_tiles, key_buf, value_buf, grad_tiles, own_lists, own_counts
    )
    buf_rows = key_grad_buf.shape[0] * TILE
    key_sum, value_sum = (
        lax.psum_scatter(
            key_grad_buf.reshape(1, buf_rows, feat_width).astype(jnp.bfloat16),
            "seq",
            scatter_dimension=1,
            tiled=True,
        ).astype(jnp.float32),
        lax.psum_scatter(
            value_grad_buf.reshape(1, buf_rows, feat_width).astype(jnp.bfloat16),
            "seq",
            scatter_dimension=1,
            tiled=True,
        ).astype(jnp.float32),
    )
    key_full = key_sum[0]
    value_full = value_sum[0]
    query_rows = query_full.reshape(tok_rows, feat_width)
    local_sums = jnp.stack(
        [
            head_squares(query_rows, head_count),
            head_squares(key_full, head_count),
            head_squares(value_full, head_count),
        ],
        axis=-1,
    )
    total_sums = lax.psum(local_sums, "seq")
    grad_features = jnp.log(total_sums / (seq_count * tok_rows * HD) + 1e-06)
    return (
        query_rows.astype(jnp.bfloat16)[None],
        key_full.astype(jnp.bfloat16)[None],
        value_full.astype(jnp.bfloat16)[None],
        grad_features[None],
    )


MESH_ID = pl.DeviceIdType.MESH
VMEM_BYTES = 58 * 1024 * 1024
NEG_BIG = -1e30
F32 = jnp.float32
BF16 = jnp.bfloat16


def dot_nt(a, b):
    return lax.dot_general(a, b, (((1,), (1,)), ((), ())), preferred_element_type=F32)


def dot_nn(a, b):
    return lax.dot_general(a, b, (((1,), (0,)), ((), ())), preferred_element_type=F32)


def fused_kernel(
    n, nh, list_ref, count_ref, q_ref, k_hbm, v_hbm, og_ref, w_hbm,
    dq_ref, dk_ref, dv_ref, feat_ref,
    k_ref, v_ref, w_ref, bias_ref, q_all, g_all, og_all, g_acc, probs, top_ref, inv_ref,
    lse_all, eps_all, part, chain, kt_ref, acc_k, acc_v, acc_q, sq_all,
    load_sem, og_send, og_recv, q_send, q_recv, g_send, g_recv, lse_send, lse_recv,
    eps_send, eps_recv, chain_send, chain_recv, sq_send, sq_recv,
):
    z = lax.axis_index("seq")
    hx = lax.axis_index("head")
    rows, width = q_ref.shape
    heads = width // HD
    feats = og_ref.shape[1]
    key_tiles = rows // TILE
    scale = HD ** (-0.5)
    scale2 = scale * math.log2(math.e)
    has_left = z > 0
    has_right = z < n - 1

    loads = [
        pltpu.make_async_copy(src, dst, load_sem.at[i])
        for i, (src, dst) in enumerate(
            ((q_ref, q_all.at[z]), (og_ref, og_all.at[hx]), (w_hbm, w_ref), (k_hbm, k_ref), (v_hbm, v_ref))
        )
    ]
    for load in loads:
        load.start()

    def remote(src, dst, ssem, rsem, axis, idx):
        return pltpu.make_async_remote_copy(
            src_ref=src, dst_ref=dst, send_sem=ssem, recv_sem=rsem,
            device_id={axis: idx}, device_id_type=MESH_ID,
        )

    def cols(h):
        return pl.ds(pl.multiple_of(h * HD, HD), HD)

    barrier = pltpu.get_barrier_semaphore()
    for i in range(1, n):
        pl.semaphore_signal(barrier, inc=1, device_id={"seq": lax.rem(z + i, n)}, device_id_type=MESH_ID)
    for i in range(1, nh):
        pl.semaphore_signal(barrier, inc=1, device_id={"head": lax.rem(hx + i, nh)}, device_id_type=MESH_ID)
    pl.semaphore_wait(barrier, n - 1 + nh - 1)

    def og_copy(i):
        return remote(og_ref, og_all.at[hx], og_send.at[i], og_recv.at[hx], "head", lax.rem(hx + i, nh))

    def og_arrival(j):
        return remote(og_all.at[j], og_all.at[j], og_send.at[0], og_recv.at[j], "head", hx)

    def q_own(way):
        return remote(q_ref, q_all.at[z], q_send.at[way, z], q_recv.at[z], "seq", z + (1 - 2 * way))

    def q_copy(b, way):
        return remote(q_all.at[b], q_all.at[b], q_send.at[way, b], q_recv.at[b], "seq", z + (1 - 2 * way))

    def g_copy(b, h, way):
        return remote(g_all.at[b, h], g_all.at[b, h], g_send.at[way, b, h], g_recv.at[b, h], "seq", z + (1 - 2 * way))

    def lse_copy(i):
        return remote(lse_all.at[z], lse_all.at[z], lse_send.at[i], lse_recv.at[z], "seq", lax.rem(z + i, n))

    def lse_arrival(d):
        return remote(lse_all.at[d], lse_all.at[d], lse_send.at[0], lse_recv.at[d], "seq", z)

    def eps_copy(h, i):
        return remote(eps_all.at[z, h], eps_all.at[z, h], eps_send.at[h, i], eps_recv.at[z, h], "seq", lax.rem(z + i, n))

    def eps_arrival(d, h):
        return remote(eps_all.at[d, h], eps_all.at[d, h], eps_send.at[h, 0], eps_recv.at[d, h], "seq", z)

    def chain_copy(b, h, way):
        slot = b if way == 0 else jnp.where(b == z - 1, n, b)
        return remote(part.at[b, h], chain.at[slot, h], chain_send.at[b, h], chain_recv.at[slot, h], "seq", z + (1 - 2 * way))

    def chain_arrival(slot, h):
        return remote(chain.at[slot, h], chain.at[slot, h], chain_send.at[0, h], chain_recv.at[slot, h], "seq", z)

    def sq_copy(i):
        return remote(sq_all.at[z], sq_all.at[z], sq_send.at[i], sq_recv.at[z], "seq", lax.rem(z + i, n))

    def sq_arrival(d):
        return remote(sq_all.at[d], sq_all.at[d], sq_send.at[0], sq_recv.at[d], "seq", z)

    def both_ways(copy_of):
        @pl.when(has_right)
        def _():
            copy_of(0)

        @pl.when(has_left)
        def _():
            copy_of(1)

    for i in range(1, nh):
        og_copy(i).start()
    both_ways(lambda way: q_own(way).start())

    tiles, slots = list_ref.shape
    for i in range(tiles):
        for j in range(key_tiles):
            bias = jnp.float32(NEG_BIG)
            for m in range(slots):
                hit = (list_ref[i, m] == z * key_tiles + j) & (m < count_ref[0, i])
                bias = jnp.where(hit, jnp.float32(0.0), bias)
            at = (i % key_tiles) * TILE
            bias_ref[i // key_tiles, j, :, at : at + TILE] = jnp.full((1, TILE), bias, F32)

    wide = 256 if width % 256 == 0 else HD

    def features_of(block, j, add):
        span = pl.ds(pl.multiple_of(j * feats, HD), feats)

        @pl.loop(0, width // wide)
        def _(c):
            at = pl.ds(pl.multiple_of(c * wide, wide), wide)
            term = dot_nt(block[...], w_ref[at, span])
            if add:
                g_acc[c] = g_acc[c] + term
            else:
                g_acc[c] = term

    for load in loads:
        load.wait()
    features_of(og_all.at[hx], hx, False)

    def q_hop(s):
        @pl.when(z - s >= 0)
        def _():
            q_copy(z - s, 0).wait_recv()

            @pl.when(has_right)
            def _():
                q_copy(z - s, 0).start()

        @pl.when(z + s < n)
        def _():
            q_copy(z + s, 1).wait_recv()

            @pl.when(has_left)
            def _():
                q_copy(z + s, 1).start()

    def softmax_rows(b):
        @pl.loop(0, heads)
        def _(h):
            ts = []
            for j in range(key_tiles):
                t = dot_nt(k_ref[j * TILE : (j + 1) * TILE, cols(h)], q_all[b, :, cols(h)])
                ts.append(t * scale2 + bias_ref[b, j])
            top = functools.reduce(jnp.maximum, [jnp.max(t, axis=0, keepdims=True) for t in ts])
            total = jnp.zeros((1, rows), F32)
            for j in range(key_tiles):
                p = jnp.exp2(ts[j] - top)
                total += jnp.sum(p, axis=0, keepdims=True)
                probs[b, h, j * TILE : (j + 1) * TILE, :] = p.astype(BF16)
            top_ref[h, b] = top
            inv_ref[h, b] = 1.0 / total
            lse_all[z, h, b] = top + jnp.log2(total)

    def softmax_at(s):
        @pl.when(z - s >= 0)
        def _():
            softmax_rows(z - s)

        @pl.when(z + s < n)
        def _():
            softmax_rows(z + s)

    @pl.loop(0, heads)
    def _(h):
        kt_ref[h] = jnp.transpose(k_ref[:, cols(h)].astype(F32)).astype(BF16)

    softmax_rows(z)
    early = min(2, n - 1)
    for s in range(1, early + 1):
        q_hop(s)
        if s < early:
            softmax_at(s)
    for i in range(1, nh):
        j = lax.rem(hx + i, nh)
        og_arrival(j).wait_recv()
        features_of(og_all.at[j], j, True)
    for h in range(heads):
        lo = h * HD
        g_all[z, h] = g_acc[lo // wide, :, lo % wide : lo % wide + HD].astype(BF16)
        both_ways(lambda way: g_copy(z, h, way).start())
    softmax_at(early)
    for s in range(early + 1, n):
        q_hop(s)
        softmax_at(s)
    for i in range(1, n):
        lse_copy(i).start()

    def g_hop(s, h):
        @pl.when((h >= 0) & (h < heads))
        def _():
            @pl.when(z - s >= 0)
            def _():
                g_copy(z - s, h, 0).wait_recv()
                if s < n - 1:
                    @pl.when(has_right)
                    def _():
                        g_copy(z - s, h, 0).start()

            @pl.when(z + s < n)
            def _():
                g_copy(z + s, h, 1).wait_recv()
                if s < n - 1:
                    @pl.when(has_left)
                    def _():
                        g_copy(z + s, h, 1).start()

    def dprobs(b, h, j):
        return dot_nt(v_ref[j * TILE : (j + 1) * TILE, cols(h)], g_all[b, h])

    def first_pass(h):
        @pl.loop(0, n)
        def _(b):
            eps = jnp.zeros((1, rows), F32)
            for j in range(key_tiles):
                p = probs[b, h, j * TILE : (j + 1) * TILE, :].astype(F32)
                eps += jnp.sum(p * dprobs(b, h, j), axis=0, keepdims=True)
            eps_all[z, h, b] = eps * inv_ref[h, b]

        for i in range(1, n):
            eps_copy(h, i).start()

    def second_pass(h):
        for i in range(1, n):
            eps_arrival(lax.rem(z + i, n), h).wait_recv()
        acc_k[...] = jnp.zeros_like(acc_k)
        acc_v[...] = jnp.zeros_like(acc_v)

        @pl.loop(0, n)
        def _(b):
            logs = [lse_all[d, h, b] for d in range(n)]
            top = functools.reduce(jnp.maximum, logs)
            log_norm = top + jnp.log2(sum(jnp.exp2(x - top) for x in logs))
            delta = sum(jnp.exp2(logs[d] - log_norm) * eps_all[d, h, b] for d in range(n))
            share = jnp.exp2(top_ref[h, b] - log_norm)
            q_b = q_all[b, :, cols(h)]
            g_b = g_all[b, h]
            dq_t = jnp.zeros((HD, rows), F32)
            for j in range(key_tiles):
                at = slice(j * TILE, (j + 1) * TILE)
                p = probs[b, h, at, :].astype(F32) * share
                ds = (p * (dprobs(b, h, j) - delta)).astype(BF16)
                acc_v[at, :] += dot_nn(p.astype(BF16), g_b)
                acc_k[at, :] += dot_nn(ds, q_b)
                dq_t += dot_nn(kt_ref[h, :, at], ds)
            part[b, h] = (dq_t * scale).astype(BF16)

        key_full = acc_k[...] * scale
        value_full = acc_v[...]
        dk_ref[:, cols(h)] = key_full.astype(BF16)
        dv_ref[:, cols(h)] = value_full.astype(BF16)
        sq_all[z, 1, h] = jnp.sum(key_full * key_full, axis=0, keepdims=True)
        sq_all[z, 2, h] = jnp.sum(value_full * value_full, axis=0, keepdims=True)

    def chain_hop(h, way):
        first = has_left if way == 0 else has_right

        @pl.when((h >= 0) & (h < heads))
        def _():
            for i in range(1, n):
                b = z + i if way == 0 else z - i

                @pl.when((b >= 0) & (b < n))
                def _():
                    @pl.when(first)
                    def _():
                        chain_arrival(b, h).wait_recv()
                        part[b, h] = (part[b, h].astype(F32) + chain[b, h].astype(F32)).astype(BF16)

                    chain_copy(b, h, way).start()

    def own_sum(h):
        @pl.when((h >= 0) & (h < heads))
        def _():
            acc_q[...] = part[z, h].astype(F32)

            @pl.when(has_left)
            def _():
                chain_arrival(z, h).wait_recv()
                acc_q[...] += chain[z, h].astype(F32)

            @pl.when(has_right)
            def _():
                chain_arrival(n, h).wait_recv()
                acc_q[...] += chain[n, h].astype(F32)

            query_full = jnp.transpose(acc_q[...])
            dq_ref[:, cols(h)] = query_full.astype(BF16)
            sq_all[z, 0, h] = jnp.sum(query_full * query_full, axis=0, keepdims=True)

    lead = max(n - 2, 0)

    @pl.loop(0, lead + heads + n)
    def _(step):
        t = step - lead
        for s in range(1, n):
            g_hop(s, t + (n - 1 - s))

        @pl.when((t >= 0) & (t < heads))
        def _():
            first_pass(t)

        @pl.when(t == 1)
        def _():
            for i in range(1, n):
                lse_arrival(lax.rem(z + i, n)).wait_recv()

        @pl.when((t >= 1) & (t <= heads))
        def _():
            second_pass(t - 1)

        chain_hop(t - 1 - z, 0)
        chain_hop(t - 1 - (n - 1 - z), 1)
        own_sum(t - 1 - jnp.maximum(z, n - 1 - z))

    for i in range(1, n):
        sq_copy(i).start()
    for i in range(1, n):
        sq_arrival(lax.rem(z + i, n)).wait_recv()
    total = functools.reduce(jnp.add, [sq_all[d] for d in range(n)])
    mean = jnp.sum(total, axis=-1, keepdims=True) / (n * rows * HD)
    logs = jnp.log(mean + 1e-06)
    lane = lax.broadcasted_iota(jnp.int32, (1, HD), 1)
    for h in range(heads):
        feat_ref[h : h + 1, :] = sum(jnp.where(lane == j, logs[j, h], 0.0) for j in range(3))

    for i in range(1, nh):
        og_copy(i).wait_send()
    for i in range(1, n):
        sq_copy(i).wait_send()
        lse_copy(i).wait_send()
    both_ways(lambda way: q_own(way).wait_send())
    for s in range(1, n - 1):
        @pl.when((z - s >= 0) & has_right)
        def _():
            q_copy(z - s, 0).wait_send()

        @pl.when((z + s < n) & has_left)
        def _():
            q_copy(z + s, 1).wait_send()

    @pl.loop(0, heads)
    def _(h):
        both_ways(lambda way: g_copy(z, h, way).wait_send())
        for s in range(1, n - 1):
            @pl.when((z - s >= 0) & has_right)
            def _():
                g_copy(z - s, h, 0).wait_send()

            @pl.when((z + s < n) & has_left)
            def _():
                g_copy(z + s, h, 1).wait_send()
        for i in range(1, n):
            eps_copy(h, i).wait_send()

            @pl.when(z + i < n)
            def _():
                chain_copy(z + i, h, 0).wait_send()

            @pl.when(z - i >= 0)
            def _():
                chain_copy(z - i, h, 1).wait_send()


def finish_kernel(dq_in, dk_in, dv_in, feat_in, dq_ref, dk_ref, dv_ref, feat_ref):
    dq_ref[...] = dq_in[...]
    dk_ref[...] = dk_in[...]
    dv_ref[...] = dv_in[...]
    feat_ref[...] = feat_in[:, : feat_ref.shape[1]]


def fused_bytes(n, nh, rows, width, feats):
    block = rows * width * 2
    kept = n * (width // HD) * rows * rows * 2
    return block * (5 + 3 * n + n + 1) + rows * feats * 2 * nh + width * feats * nh * 2 + 2 * block + kept


def per_device(query_states, key_states, value_states, output_grad, w_out, key_list, key_count):
    n = lax.axis_size("seq")
    nh = lax.axis_size("head")
    rows, width = query_states.shape[1:]
    feats = output_grad.shape[2]
    if n < 2 or fused_bytes(n, nh, rows, width, feats) > VMEM_BYTES * 3 // 4:
        return gathered_plan(
            query_states, key_states, value_states, output_grad, w_out, key_list, key_count
        )
    heads = width // HD
    key_tiles = rows // TILE
    wide = 256 if width % 256 == 0 else HD
    vmem = pl.BlockSpec(memory_space=pltpu.VMEM)
    dma = pltpu.SemaphoreType.DMA
    block = jax.ShapeDtypeStruct((rows, width), BF16)
    dq, dk, dv, feat = pl.pallas_call(
        functools.partial(fused_kernel, n, nh),
        out_shape=[block, block, block, jax.ShapeDtypeStruct((heads, HD), F32)],
        in_specs=[pl.BlockSpec(memory_space=pltpu.SMEM)] * 2 + [pl.BlockSpec(memory_space=pl.ANY)] * 5,
        out_specs=[vmem] * 4,
        scratch_shapes=[
            pltpu.VMEM((rows, width), BF16),
            pltpu.VMEM((rows, width), BF16),
            pltpu.VMEM((width, feats * nh), BF16),
            pltpu.VMEM((n, key_tiles, 1, rows), F32),
            pltpu.VMEM((n, rows, width), BF16),
            pltpu.VMEM((n, heads, rows, HD), BF16),
            pltpu.VMEM((nh, rows, feats), BF16),
            pltpu.VMEM((width // wide, rows, wide), F32),
            pltpu.VMEM((n, heads, rows, rows), BF16),
            pltpu.VMEM((heads, n, 1, rows), F32),
            pltpu.VMEM((heads, n, 1, rows), F32),
            pltpu.VMEM((n, heads, n, 1, rows), F32),
            pltpu.VMEM((n, heads, n, 1, rows), F32),
            pltpu.VMEM((n, heads, HD, rows), BF16),
            pltpu.VMEM((n + 1, heads, HD, rows), BF16),
            pltpu.VMEM((heads, HD, rows), BF16),
            pltpu.VMEM((rows, HD), F32),
            pltpu.VMEM((rows, HD), F32),
            pltpu.VMEM((HD, rows), F32),
            pltpu.VMEM((n, 3, heads, 1, HD), F32),
            dma((5,)),
            dma((nh,)), dma((nh,)),
            dma((2, n)), dma((n,)),
            dma((2, n, heads)), dma((n, heads)),
            dma((n,)), dma((n,)),
            dma((heads, n)), dma((n, heads)),
            dma((n, heads)), dma((n + 1, heads)),
            dma((n,)), dma((n,)),
        ],
        compiler_params=pltpu.CompilerParams(
            collective_id=0, has_side_effects=True, vmem_limit_bytes=VMEM_BYTES
        ),
        cost_estimate=pl.CostEstimate(
            flops=14 * rows * rows * n * width + 2 * rows * width * feats * nh,
            bytes_accessed=16 * rows * width,
            transcendentals=2 * rows * rows * n * heads,
        ),
    )(key_list[0], key_count, query_states[0], key_states[0], value_states[0], output_grad[0], w_out)
    dq, dk, dv, grad_features = pl.pallas_call(
        finish_kernel,
        out_shape=[block, block, block, jax.ShapeDtypeStruct((heads, 3), F32)],
        in_specs=[vmem] * 4,
        out_specs=[vmem] * 4,
    )(dq, dk, dv, feat)
    return dq[None], dk[None], dv[None], grad_features[None]


def solution(mesh):
    in_specs = (
        P(("grp", "clip"), "seq", "head"),
        P(("grp", "clip"), "seq", "head"),
        P(("grp", "clip"), "seq", "head"),
        P(("grp", "clip"), "seq", "head"),
        P("head", None),
        P(("grp", "clip"), None, None),
        P(("grp", "clip"), None),
    )
    out_specs = (
        P(("grp", "clip"), "seq", "head"),
        P(("grp", "clip"), "seq", "head"),
        P(("grp", "clip"), "seq", "head"),
        P(("grp", "clip"), "head", None),
    )
    return jax.shard_map(
        per_device, mesh=mesh, in_specs=in_specs, out_specs=out_specs, check_vma=False
    )
```

```python
import functools
import math

import jax
import jax.numpy as jnp
from jax import lax
from jax.experimental import pallas as pl
from jax.experimental.pallas import tpu as pltpu
from jax.sharding import PartitionSpec as P

HD = 128
TILE = 256


def attend(query_tiles, key_buf, value_buf, grad_tiles, buf_slots, counts):
    score_scale = HD ** (-0.5)
    tile_count, tile_rows, feat_width = query_tiles.shape
    slot_count = buf_slots.shape[1]
    key_span = slot_count * tile_rows
    buf_tiles = key_buf.shape[0]
    key_sel = key_buf[buf_slots].reshape(tile_count, key_span, feat_width)
    value_sel = value_buf[buf_slots].reshape(tile_count, key_span, feat_width)
    allowed = jnp.arange(key_span)[None, :] // tile_rows < counts[:, None]

    def head_step(head_idx, carried):
        query_acc, key_acc, value_acc = carried
        col_start = head_idx * HD
        query_head = lax.dynamic_slice_in_dim(query_tiles, col_start, HD, 2)
        key_head = lax.dynamic_slice_in_dim(key_sel, col_start, HD, 2)
        value_head = lax.dynamic_slice_in_dim(value_sel, col_start, HD, 2)
        grad_head = lax.dynamic_slice_in_dim(grad_tiles, col_start, HD, 2)
        scores = (
            jnp.einsum("iqe,ike->iqk", query_head, key_head, preferred_element_type=jnp.float32)
            * score_scale
        )
        scores = jnp.where(allowed[:, None, :], scores, -jnp.inf)
        row_max = jnp.max(scores, axis=-1, keepdims=True)
        log_norm = row_max + jnp.log(jnp.sum(jnp.exp(scores - row_max), axis=-1, keepdims=True))
        weights = jnp.exp(scores - log_norm)
        weights_b = weights.astype(jnp.bfloat16)
        attn_out = jnp.einsum(
            "iqk,ike->iqe", weights_b, value_head, preferred_element_type=jnp.float32
        ).astype(jnp.bfloat16)
        row_delta = jnp.sum(
            grad_head.astype(jnp.float32) * attn_out.astype(jnp.float32), axis=-1, keepdims=True
        )
        dprob = jnp.einsum(
            "iqe,ike->iqk", grad_head, value_head, preferred_element_type=jnp.float32
        )
        dscore = (weights * (dprob - row_delta)).astype(jnp.bfloat16)
        query_head_grad = score_scale * jnp.einsum(
            "iqk,ike->iqe", dscore, key_head, preferred_element_type=jnp.float32
        )
        key_head_grad = score_scale * jnp.einsum(
            "iqk,iqe->ike", dscore, query_head, preferred_element_type=jnp.float32
        )
        value_head_grad = jnp.einsum(
            "iqk,iqe->ike", weights_b, grad_head, preferred_element_type=jnp.float32
        )
        query_acc = lax.dynamic_update_slice_in_dim(query_acc, query_head_grad, col_start, 2)
        key_acc = lax.dynamic_update_slice_in_dim(key_acc, key_head_grad, col_start, 2)
        value_acc = lax.dynamic_update_slice_in_dim(value_acc, value_head_grad, col_start, 2)
        return (query_acc, key_acc, value_acc)

    start_state = (
        jnp.zeros((tile_count, tile_rows, feat_width), jnp.float32),
        jnp.zeros((tile_count, key_span, feat_width), jnp.float32),
        jnp.zeros((tile_count, key_span, feat_width), jnp.float32),
    )
    query_full, key_sel_grad, value_sel_grad = lax.fori_loop(
        0, feat_width // HD, head_step, start_state
    )
    live_slot = jnp.arange(slot_count)[None, :] < counts[:, None]
    routing = (
        (buf_slots[:, :, None] == jnp.arange(buf_tiles)[None, None, :]) & live_slot[:, :, None]
    ).astype(jnp.float32)
    key_grad_buf = jnp.einsum(
        "imb,imr->br",
        routing,
        key_sel_grad.reshape(tile_count, slot_count, tile_rows * feat_width),
        precision=lax.Precision.HIGHEST,
    )
    value_grad_buf = jnp.einsum(
        "imb,imr->br",
        routing,
        value_sel_grad.reshape(tile_count, slot_count, tile_rows * feat_width),
        precision=lax.Precision.HIGHEST,
    )
    return (
        query_full,
        key_grad_buf.reshape(buf_tiles, tile_rows, feat_width),
        value_grad_buf.reshape(buf_tiles, tile_rows, feat_width),
    )


def head_squares(grads_full, head_count):
    rows = grads_full.reshape(-1, head_count, HD)
    return jnp.sum(rows * rows, axis=(0, 2))


def gathered_plan(query_states, key_states, value_states, output_grad, w_out, key_list, key_count):
    seq_count = lax.axis_size("seq")
    seq_index = lax.axis_index("seq")
    tok_rows = query_states.shape[1]
    feat_width = query_states.shape[2]
    head_count = feat_width // HD
    tile_count = tok_rows // TILE
    first_tile = seq_index * tile_count
    own_lists = lax.dynamic_slice_in_dim(key_list[0], first_tile, tile_count, 0)
    own_counts = lax.dynamic_slice_in_dim(key_count[0], first_tile, tile_count, 0)
    grad_out = lax.dot_general(
        lax.all_gather(output_grad, "head", axis=2, tiled=True)[0],
        w_out,
        (((1,), (1,)), ((), ())),
        preferred_element_type=jnp.float32,
    ).astype(jnp.bfloat16)
    query_tiles = query_states[0].reshape(tile_count, TILE, feat_width)
    grad_tiles = grad_out.reshape(tile_count, TILE, feat_width)
    key_whole, value_whole = (
        lax.all_gather(key_states, "seq", axis=1, tiled=True),
        lax.all_gather(value_states, "seq", axis=1, tiled=True),
    )
    key_buf = key_whole[0].reshape(-1, TILE, feat_width)
    value_buf = value_whole[0].reshape(-1, TILE, feat_width)
    query_full, key_grad_buf, value_grad_buf = attend(
        query_tiles, key_buf, value_buf, grad_tiles, own_lists, own_counts
    )
    buf_rows = key_grad_buf.shape[0] * TILE
    key_sum, value_sum = (
        lax.psum_scatter(
            key_grad_buf.reshape(1, buf_rows, feat_width).astype(jnp.bfloat16),
            "seq",
            scatter_dimension=1,
            tiled=True,
        ).astype(jnp.float32),
        lax.psum_scatter(
            value_grad_buf.reshape(1, buf_rows, feat_width).astype(jnp.bfloat16),
            "seq",
            scatter_dimension=1,
            tiled=True,
        ).astype(jnp.float32),
    )
    key_full = key_sum[0]
    value_full = value_sum[0]
    query_rows = query_full.reshape(tok_rows, feat_width)
    local_sums = jnp.stack(
        [
            head_squares(query_rows, head_count),
            head_squares(key_full, head_count),
            head_squares(value_full, head_count),
        ],
        axis=-1,
    )
    total_sums = lax.psum(local_sums, "seq")
    grad_features = jnp.log(total_sums / (seq_count * tok_rows * HD) + 1e-06)
    return (
        query_rows.astype(jnp.bfloat16)[None],
        key_full.astype(jnp.bfloat16)[None],
        value_full.astype(jnp.bfloat16)[None],
        grad_features[None],
    )


MESH_ID = pl.DeviceIdType.MESH
VMEM_BYTES = 58 * 1024 * 1024
NEG_BIG = -1e30
F32 = jnp.float32
BF16 = jnp.bfloat16


def dot_nt(a, b):
    return lax.dot_general(a, b, (((1,), (1,)), ((), ())), preferred_element_type=F32)


def dot_nn(a, b):
    return lax.dot_general(a, b, (((1,), (0,)), ((), ())), preferred_element_type=F32)


def fused_kernel(
    n, nh, gc, list_ref, count_ref, q_ref, k_hbm, v_hbm, og_ref, w_hbm,
    dq_ref, dk_ref, dv_ref, feat_ref,
    k_ref, v_ref, w_ref, bias_ref, q_all, g_all, og_all, g_acc, probs, top_ref, inv_ref,
    lse_all, eps_all, part, chain, kt_ref, acc_k, acc_v, acc_q, sq_all,
    guest_out, guest_in, guest_send, guest_recv, back_send, back_recv, load_sem, og_send, og_recv, q_send, q_recv, g_send, g_recv, lse_send, lse_recv,
    eps_send, eps_recv, chain_send, chain_recv, sq_send, sq_recv,
):
    z = lax.axis_index("seq")
    hx = lax.axis_index("head")
    rows, width = q_ref.shape
    heads = width // HD
    feats = og_ref.shape[1]
    key_tiles = rows // TILE
    scale = HD ** (-0.5)
    scale2 = scale * math.log2(math.e)
    has_left = z > 0
    has_right = z < n - 1
    gw = gc * HD
    is_end = (z == 0) | (z == n - 1)
    host_low, host_high = z == 1, z == n - 2
    is_host = (host_low | host_high) if gc else z < 0
    guest = jnp.where(host_low, 0, n - 1)
    host_of = jnp.where(z == 0, 1, n - 2)

    def inner(d):
        return (d > 0) & (d < n - 1)

    def may_go(way, guest_part):
        to = z + (1 - 2 * way)
        return inner(to) if guest_part else (to >= 0) & (to < n)

    loads = [
        pltpu.make_async_copy(src, dst, load_sem.at[i])
        for i, (src, dst) in enumerate(
            ((q_ref, q_all.at[z]), (og_ref, og_all.at[hx]), (w_hbm, w_ref), (k_hbm, k_ref.at[:, 0:width]), (v_hbm, v_ref.at[:, 0:width]))
        )
    ]
    for load in loads:
        load.start()

    def remote(src, dst, ssem, rsem, axis, idx):
        return pltpu.make_async_remote_copy(
            src_ref=src, dst_ref=dst, send_sem=ssem, recv_sem=rsem,
            device_id={axis: idx}, device_id_type=MESH_ID,
        )

    def cols(h):
        return pl.ds(pl.multiple_of(h * HD, HD), HD)

    barrier = pltpu.get_barrier_semaphore()
    for i in range(1, n):
        pl.semaphore_signal(barrier, inc=1, device_id={"seq": lax.rem(z + i, n)}, device_id_type=MESH_ID)
    for i in range(1, nh):
        pl.semaphore_signal(barrier, inc=1, device_id={"head": lax.rem(hx + i, nh)}, device_id_type=MESH_ID)
    pl.semaphore_wait(barrier, n - 1 + nh - 1)

    def og_copy(i):
        return remote(og_ref, og_all.at[hx], og_send.at[i], og_recv.at[hx], "head", lax.rem(hx + i, nh))

    def og_arrival(j):
        return remote(og_all.at[j], og_all.at[j], og_send.at[0], og_recv.at[j], "head", hx)

    q_parts = [(0, gw), (gw, width - gw)] if gc else [(0, width)]

    def q_own(way, p):
        at = pl.ds(*q_parts[p])
        return remote(q_ref.at[:, at], q_all.at[z, :, at], q_send.at[way, z, p], q_recv.at[z, p], "seq", z + (1 - 2 * way))

    def q_copy(b, way, p):
        ref = q_all.at[b, :, pl.ds(*q_parts[p])]
        return remote(ref, ref, q_send.at[way, b, p], q_recv.at[b, p], "seq", z + (1 - 2 * way))

    def lend(i):
        src, dst = ((k_hbm, k_ref), (v_hbm, v_ref))[i]
        return remote(src.at[:, 0:gw], dst.at[:, width : width + gw], guest_send.at[i], guest_recv.at[i], "seq", host_of)

    def lent(i):
        ref = (k_ref, v_ref)[i].at[:, width : width + gw]
        return remote(ref, ref, guest_send.at[i], guest_recv.at[i], "seq", z)

    def back_copy(h):
        return remote(guest_out.at[h], guest_in.at[h], back_send.at[h], back_recv.at[h], "seq", guest)

    def back_arrival(h):
        return remote(guest_in.at[h], guest_in.at[h], back_send.at[h], back_recv.at[h], "seq", z)

    def g_copy(b, h, way):
        return remote(g_all.at[b, h], g_all.at[b, h], g_send.at[way, b, h], g_recv.at[b, h], "seq", z + (1 - 2 * way))

    def lse_ref(d, p):
        return lse_all.at[d, 0:gc] if p else lse_all.at[d, gc:heads]

    def lse_copy(d, i, p, k):
        return remote(lse_ref(d, p), lse_ref(d, p), lse_send.at[i, k], lse_recv.at[d, p], "seq", lax.rem(z + i, n))

    def lse_arrival(d, p):
        return remote(lse_ref(d, p), lse_ref(d, p), lse_send.at[0, 0], lse_recv.at[d, p], "seq", z)

    def eps_copy(d, h, i, k):
        return remote(eps_all.at[d, h], eps_all.at[d, h], eps_send.at[h, i, k], eps_recv.at[d, h], "seq", lax.rem(z + i, n))

    def eps_arrival(d, h):
        return remote(eps_all.at[d, h], eps_all.at[d, h], eps_send.at[h, 0, 0], eps_recv.at[d, h], "seq", z)

    def lse_sends(act):
        for i in range(1, n):
            act(lse_copy(z, i, 0, 0))
            if gc:
                @pl.when(inner(z) & inner(lax.rem(z + i, n)))
                def _():
                    act(lse_copy(z, i, 1, 1))

                    @pl.when(is_host)
                    def _():
                        act(lse_copy(guest, i, 1, 2))

    def eps_sends(h, act):
        for i in range(1, n):
            @pl.when((h >= gc) | (inner(z) & inner(lax.rem(z + i, n))))
            def _():
                act(eps_copy(z, h, i, 0))

            @pl.when((h < gc) & is_host & inner(lax.rem(z + i, n)))
            def _():
                act(eps_copy(guest, h, i, 1))

    def chain_copy(b, h, way):
        slot = b if way == 0 else jnp.where(b == z - 1, n, b)
        return remote(part.at[b, h], chain.at[slot, h], chain_send.at[b, h], chain_recv.at[slot, h], "seq", z + (1 - 2 * way))

    def chain_arrival(slot, h):
        return remote(chain.at[slot, h], chain.at[slot, h], chain_send.at[0, h], chain_recv.at[slot, h], "seq", z)

    def sq_copy(i):
        return remote(sq_all.at[z], sq_all.at[z], sq_send.at[i], sq_recv.at[z], "seq", lax.rem(z + i, n))

    def sq_arrival(d):
        return remote(sq_all.at[d], sq_all.at[d], sq_send.at[0], sq_recv.at[d], "seq", z)

    def q_own_all(act):
        for p in range(len(q_parts)):
            for way in range(2):
                @pl.when(may_go(way, gc > 0 and p == 0))
                def _():
                    act(q_own(way, p))

    def q_on(s, act):
        for way, b in ((0, z - s), (1, z + s)):
            for p in range(len(q_parts)):
                @pl.when((b >= 0) & (b < n) & may_go(way, gc > 0 and p == 0))
                def _():
                    act(q_copy(b, way, p))

    def g_sends(b, h, way, act):
        @pl.when((b >= 0) & (b < n) & may_go(way, False) & ((h >= gc) | may_go(way, True)))
        def _():
            act(g_copy(b, h, way))

    for i in range(1, nh):
        og_copy(i).start()
    q_own_all(lambda c: c.start())
    if gc:
        @pl.when(is_end)
        def _():
            lend(0).start()
            lend(1).start()

    tiles, slots = list_ref.shape
    for i in range(tiles):
        for j in range(key_tiles):
            at = (i % key_tiles) * TILE
            for k, owner in enumerate((z, guest) if gc else (z,)):
                bias = jnp.float32(NEG_BIG)
                for m in range(slots):
                    hit = (list_ref[i, m] == owner * key_tiles + j) & (m < count_ref[0, i])
                    bias = jnp.where(hit, jnp.float32(0.0), bias)
                bias_ref[k, i // key_tiles, j, :, at : at + TILE] = jnp.full((1, TILE), bias, F32)

    wide = 256 if width % 256 == 0 else HD

    def features_of(block, j, add):
        span = pl.ds(pl.multiple_of(j * feats, HD), feats)

        @pl.loop(0, width // wide)
        def _(c):
            at = pl.ds(pl.multiple_of(c * wide, wide), wide)
            term = dot_nt(block[...], w_ref[at, span])
            if add:
                g_acc[c] = g_acc[c] + term
            else:
                g_acc[c] = term

    for load in loads:
        load.wait()
    features_of(og_all.at[hx], hx, False)

    def q_hop(s):
        for way, b in ((0, z - s), (1, z + s)):
            @pl.when((b >= 0) & (b < n))
            def _():
                for p in range(len(q_parts)):
                    @pl.when(inner(z) if gc > 0 and p == 0 else z >= 0)
                    def _():
                        q_copy(b, way, p).wait_recv()

                        @pl.when(may_go(way, gc > 0 and p == 0))
                        def _():
                            q_copy(b, way, p).start()

    first_head = jnp.where(is_end, gc, 0)

    def softmax_rows(b, low, high):
        @pl.loop(low, high)
        def _(v):
            mine = v < heads
            h = jnp.where(mine, v, v - heads)
            ts = []
            for j in range(key_tiles):
                t = dot_nt(k_ref[j * TILE : (j + 1) * TILE, cols(v)], q_all[b, :, cols(h)])
                ts.append(t * scale2 + bias_ref[jnp.where(mine, 0, 1), b, j])
            top = functools.reduce(jnp.maximum, [jnp.max(t, axis=0, keepdims=True) for t in ts])
            total = jnp.zeros((1, rows), F32)
            for j in range(key_tiles):
                p = jnp.exp2(ts[j] - top)
                total += jnp.sum(p, axis=0, keepdims=True)
                probs[b, v, j * TILE : (j + 1) * TILE, :] = p.astype(BF16)
            top_ref[v, b] = top
            inv_ref[v, b] = 1.0 / total
            lse_all[jnp.where(mine, z, guest), h, b] = top + jnp.log2(total)

    def softmax_at(s):
        @pl.when(z - s >= 0)
        def _():
            softmax_rows(z - s, first_head, heads)

        @pl.when(z + s < n)
        def _():
            softmax_rows(z + s, first_head, heads)

    @pl.loop(0, heads)
    def _(h):
        kt_ref[h] = jnp.transpose(k_ref[:, cols(h)].astype(F32)).astype(BF16)

    softmax_rows(z, first_head, heads)
    early = min(2, n - 1)
    for s in range(1, early + 1):
        q_hop(s)
        if s < early:
            softmax_at(s)
    for i in range(1, nh):
        j = lax.rem(hx + i, nh)
        og_arrival(j).wait_recv()
        features_of(og_all.at[j], j, True)
    for h in range(heads):
        lo = h * HD
        g_all[z, h] = g_acc[lo // wide, :, lo % wide : lo % wide + HD].astype(BF16)
        for way in range(2):
            g_sends(z, h, way, lambda c: c.start())
    softmax_at(early)
    for s in range(early + 1, n):
        q_hop(s)
        softmax_at(s)
    if gc:
        @pl.when(is_host)
        def _():
            lent(0).wait_recv()
            lent(1).wait_recv()

            @pl.loop(heads, heads + gc)
            def _(v):
                kt_ref[v] = jnp.transpose(k_ref[:, cols(v)].astype(F32)).astype(BF16)

            @pl.loop(0, n)
            def _(b):
                softmax_rows(b, heads, heads + gc)

    lse_sends(lambda c: c.start())

    def g_hop(s, h):
        for way, b in ((0, z - s), (1, z + s)):
            @pl.when((h >= 0) & (h < heads) & (b >= 0) & (b < n) & ((h >= gc) | inner(z)))
            def _():
                g_copy(b, h, way).wait_recv()
                if s < n - 1:
                    g_sends(b, h, way, lambda c: c.start())

    def dprobs(b, v, h, j):
        return dot_nt(v_ref[j * TILE : (j + 1) * TILE, cols(v)], g_all[b, h])

    def holders(h):
        return jnp.where(h < gc, jnp.where(is_end, 0, jnp.where(is_host, 2, 1)), 1)

    def first_pass(h):
        @pl.loop(0, holders(h))
        def _(k):
            v = h + k * heads
            owner = jnp.where(k == 0, z, guest)

            @pl.loop(0, n)
            def _(b):
                eps = jnp.zeros((1, rows), F32)
                for j in range(key_tiles):
                    p = probs[b, v, j * TILE : (j + 1) * TILE, :].astype(F32)
                    eps += jnp.sum(p * dprobs(b, v, h, j), axis=0, keepdims=True)
                eps_all[owner, h, b] = eps * inv_ref[v, b]

        eps_sends(h, lambda c: c.start())

    def second_pass(h):
        for i in range(1, n):
            d = lax.rem(z + i, n)
            skip = (d == guest) & is_host

            @pl.when((h >= gc) | (inner(z) & jnp.logical_not(skip)))
            def _():
                eps_arrival(d, h).wait_recv()

        for b in range(n):
            part[b, h] = jnp.zeros((HD, rows), BF16)

        @pl.loop(0, holders(h))
        def _(k):
            v = h + k * heads
            acc_k[...] = jnp.zeros_like(acc_k)
            acc_v[...] = jnp.zeros_like(acc_v)

            @pl.loop(0, n)
            def _(b):
                logs = [lse_all[d, h, b] for d in range(n)]
                top = functools.reduce(jnp.maximum, logs)
                log_norm = top + jnp.log2(sum(jnp.exp2(x - top) for x in logs))
                delta = sum(jnp.exp2(logs[d] - log_norm) * eps_all[d, h, b] for d in range(n))
                share = jnp.exp2(top_ref[v, b] - log_norm)
                q_b = q_all[b, :, cols(h)]
                g_b = g_all[b, h]
                dq_t = jnp.zeros((HD, rows), F32)
                for j in range(key_tiles):
                    at = slice(j * TILE, (j + 1) * TILE)
                    p = probs[b, v, at, :].astype(F32) * share
                    ds = (p * (dprobs(b, v, h, j) - delta)).astype(BF16)
                    acc_v[at, :] += dot_nn(p.astype(BF16), g_b)
                    acc_k[at, :] += dot_nn(ds, q_b)
                    dq_t += dot_nn(kt_ref[v, :, at], ds)
                part[b, h] = (part[b, h].astype(F32) + dq_t * scale).astype(BF16)

            key_full = acc_k[...] * scale
            value_full = acc_v[...]

            @pl.when(k == 0)
            def _():
                dk_ref[:, cols(h)] = key_full.astype(BF16)
                dv_ref[:, cols(h)] = value_full.astype(BF16)
                sq_all[z, 1, h] = jnp.sum(key_full * key_full, axis=0, keepdims=True)
                sq_all[z, 2, h] = jnp.sum(value_full * value_full, axis=0, keepdims=True)

            if gc:
                @pl.when(k == 1)
                def _():
                    guest_out[h, 0] = key_full.astype(BF16)
                    guest_out[h, 1] = value_full.astype(BF16)
                    back_copy(h).start()

    def take_back(h):
        @pl.when((h >= 0) & (h < gc) & is_end)
        def _():
            back_arrival(h).wait_recv()
            for i, ref in enumerate((dk_ref, dv_ref)):
                ref[:, cols(h)] = guest_in[h, i]
                full = guest_in[h, i].astype(F32)
                sq_all[z, i + 1, h] = jnp.sum(full * full, axis=0, keepdims=True)

    def comes(h, way):
        far = z if way == 0 else n - 1 - z
        return far > jnp.where(h < gc, 1, 0)

    def chain_sends(h, way, act):
        for i in reversed(range(1, n)):
            b = z + i if way == 0 else z - i

            @pl.when((b >= 0) & (b < n) & ((h >= gc) | inner(z)))
            def _():
                act(b)

    def chain_hop(h, way):
        def hop(b):
            @pl.when(comes(h, way))
            def _():
                chain_arrival(b, h).wait_recv()
                part[b, h] = (part[b, h].astype(F32) + chain[b, h].astype(F32)).astype(BF16)

            chain_copy(b, h, way).start()

        @pl.when((h >= 0) & (h < heads))
        def _():
            chain_sends(h, way, hop)

    def own_sum(h):
        @pl.when((h >= 0) & (h < heads))
        def _():
            acc_q[...] = jnp.zeros_like(acc_q)

            @pl.when((h >= gc) | inner(z))
            def _():
                acc_q[...] = part[z, h].astype(F32)

            for way, slot in ((0, z), (1, n)):
                @pl.when(comes(h, way))
                def _():
                    chain_arrival(slot, h).wait_recv()
                    acc_q[...] += chain[slot, h].astype(F32)

            query_full = jnp.transpose(acc_q[...])
            dq_ref[:, cols(h)] = query_full.astype(BF16)
            sq_all[z, 0, h] = jnp.sum(query_full * query_full, axis=0, keepdims=True)

    lead = max(n - 2, 0)

    @pl.loop(0, lead + heads + n)
    def _(step):
        t = step - lead
        for s in range(1, n):
            g_hop(s, t + (n - 1 - s))

        @pl.when((t >= 0) & (t < heads))
        def _():
            first_pass(t)

        @pl.when(t == 1)
        def _():
            for i in range(1, n):
                d = lax.rem(z + i, n)
                lse_arrival(d, 0).wait_recv()
                if gc:
                    skip = (d == guest) & is_host

                    @pl.when(inner(z) & jnp.logical_not(skip))
                    def _():
                        lse_arrival(d, 1).wait_recv()

        @pl.when((t >= 1) & (t <= heads))
        def _():
            second_pass(t - 1)

        chain_hop(t - 1 - z, 0)
        chain_hop(t - 1 - (n - 1 - z), 1)
        own_sum(t - 1 - jnp.maximum(z, n - 1 - z))
        if gc:
            take_back(t - 3)

    for i in range(1, n):
        sq_copy(i).start()
    for i in range(1, n):
        sq_arrival(lax.rem(z + i, n)).wait_recv()
    total = functools.reduce(jnp.add, [sq_all[d] for d in range(n)])
    mean = jnp.sum(total, axis=-1, keepdims=True) / (n * rows * HD)
    logs = jnp.log(mean + 1e-06)
    lane = lax.broadcasted_iota(jnp.int32, (1, HD), 1)
    for j in range(3):
        feat_ref[j] = sum(jnp.where(lane == h, logs[j, h], 0.0) for h in range(heads))

    for i in range(1, nh):
        og_copy(i).wait_send()
    for i in range(1, n):
        sq_copy(i).wait_send()
    lse_sends(lambda c: c.wait_send())
    q_own_all(lambda c: c.wait_send())
    for s in range(1, n - 1):
        q_on(s, lambda c: c.wait_send())
    if gc:
        @pl.when(is_end)
        def _():
            lend(0).wait_send()
            lend(1).wait_send()

    @pl.loop(0, heads)
    def _(h):
        for way in range(2):
            for s in range(n - 1):
                b = z - s if way == 0 else z + s

                @pl.when((h >= gc) | inner(z) | (b == z))
                def _():
                    g_sends(b, h, way, lambda c: c.wait_send())

            chain_sends(h, way, lambda b: chain_copy(b, h, way).wait_send())
        eps_sends(h, lambda c: c.wait_send())
        if gc:
            @pl.when((h < gc) & is_host)
            def _():
                back_copy(h).wait_send()


def finish_kernel(dq_in, dk_in, dv_in, feat_in, dq_ref, dk_ref, dv_ref, feat_ref):
    dq_ref[...] = dq_in[...]
    dk_ref[...] = dk_in[...]
    dv_ref[...] = dv_in[...]
    feat_ref[...] = feat_in[:, :, : feat_ref.shape[2]]


def fused_bytes(n, nh, rows, width, feats):
    block = rows * width * 2
    kept = n * (width // HD) * rows * rows * 3
    return block * (5 + 3 * n + n + 1) + rows * feats * 2 * nh + width * feats * nh * 2 + 2 * block + kept


def per_device(query_states, key_states, value_states, output_grad, w_out, key_list, key_count):
    n = lax.axis_size("seq")
    nh = lax.axis_size("head")
    rows, width = query_states.shape[1:]
    feats = output_grad.shape[2]
    if n < 2 or fused_bytes(n, nh, rows, width, feats) > VMEM_BYTES * 3 // 4:
        return gathered_plan(
            query_states, key_states, value_states, output_grad, w_out, key_list, key_count
        )
    heads = width // HD
    key_tiles = rows // TILE
    wide = 256 if width % 256 == 0 else HD
    gc = heads // 3 if n >= 4 else 0
    gn = max(gc, 1)
    vmem = pl.BlockSpec(memory_space=pltpu.VMEM)
    dma = pltpu.SemaphoreType.DMA
    block = jax.ShapeDtypeStruct((rows, width), BF16)
    dq, dk, dv, feat = pl.pallas_call(
        functools.partial(fused_kernel, n, nh, gc),
        out_shape=[block, block, block, jax.ShapeDtypeStruct((3, 1, HD), F32)],
        in_specs=[pl.BlockSpec(memory_space=pltpu.SMEM)] * 2 + [pl.BlockSpec(memory_space=pl.ANY)] * 5,
        out_specs=[vmem] * 4,
        scratch_shapes=[
            pltpu.VMEM((rows, width + gc * HD), BF16),
            pltpu.VMEM((rows, width + gc * HD), BF16),
            pltpu.VMEM((width, feats * nh), BF16),
            pltpu.VMEM((2, n, key_tiles, 1, rows), F32),
            pltpu.VMEM((n, rows, width), BF16),
            pltpu.VMEM((n, heads, rows, HD), BF16),
            pltpu.VMEM((nh, rows, feats), BF16),
            pltpu.VMEM((width // wide, rows, wide), F32),
            pltpu.VMEM((n, heads + gc, rows, rows), BF16),
            pltpu.VMEM((heads + gc, n, 1, rows), F32),
            pltpu.VMEM((heads + gc, n, 1, rows), F32),
            pltpu.VMEM((n, heads, n, 1, rows), F32),
            pltpu.VMEM((n, heads, n, 1, rows), F32),
            pltpu.VMEM((n, heads, HD, rows), BF16),
            pltpu.VMEM((n + 1, heads, HD, rows), BF16),
            pltpu.VMEM((heads + gc, HD, rows), BF16),
            pltpu.VMEM((rows, HD), F32),
            pltpu.VMEM((rows, HD), F32),
            pltpu.VMEM((HD, rows), F32),
            pltpu.VMEM((n, 3, heads, 1, HD), F32),
            pltpu.VMEM((gn, 2, rows, HD), BF16),
            pltpu.VMEM((gn, 2, rows, HD), BF16),
            dma((2,)), dma((2,)), dma((gn,)), dma((gn,)),
            dma((5,)),
            dma((nh,)), dma((nh,)),
            dma((2, n, 2)), dma((n, 2)),
            dma((2, n, heads)), dma((n, heads)),
            dma((n, 3)), dma((n, 2)),
            dma((heads, n, 2)), dma((n, heads)),
            dma((n, heads)), dma((n + 1, heads)),
            dma((n,)), dma((n,)),
        ],
        compiler_params=pltpu.CompilerParams(
            collective_id=0, has_side_effects=True, vmem_limit_bytes=VMEM_BYTES
        ),
        cost_estimate=pl.CostEstimate(
            flops=14 * rows * rows * n * width + 2 * rows * width * feats * nh,
            bytes_accessed=16 * rows * width,
            transcendentals=2 * rows * rows * n * heads,
        ),
    )(key_list[0], key_count, query_states[0], key_states[0], value_states[0], output_grad[0], w_out)
    dq, dk, dv, grad_features = pl.pallas_call(
        finish_kernel,
        out_shape=[block, block, block, jax.ShapeDtypeStruct((3, 1, heads), F32)],
        in_specs=[vmem] * 4,
        out_specs=[vmem] * 4,
    )(dq, dk, dv, feat)
    return dq[None], dk[None], dv[None], jnp.transpose(grad_features, (1, 2, 0))


def solution(mesh):
    in_specs = (
        P(("grp", "clip"), "seq", "head"),
        P(("grp", "clip"), "seq", "head"),
        P(("grp", "clip"), "seq", "head"),
        P(("grp", "clip"), "seq", "head"),
        P("head", None),
        P(("grp", "clip"), None, None),
        P(("grp", "clip"), None),
    )
    out_specs = (
        P(("grp", "clip"), "seq", "head"),
        P(("grp", "clip"), "seq", "head"),
        P(("grp", "clip"), "seq", "head"),
        P(("grp", "clip"), "head", None),
    )
    return jax.shard_map(
        per_device, mesh=mesh, in_specs=in_specs, out_specs=out_specs, check_vma=False
    )
```

```python
import functools
import math

import jax
import jax.numpy as jnp
from jax import lax
from jax.experimental import pallas as pl
from jax.experimental.pallas import tpu as pltpu
from jax.sharding import PartitionSpec as P

HD = 128
TILE = 256


def attend(query_tiles, key_buf, value_buf, grad_tiles, buf_slots, counts):
    score_scale = HD ** (-0.5)
    tile_count, tile_rows, feat_width = query_tiles.shape
    slot_count = buf_slots.shape[1]
    key_span = slot_count * tile_rows
    buf_tiles = key_buf.shape[0]
    key_sel = key_buf[buf_slots].reshape(tile_count, key_span, feat_width)
    value_sel = value_buf[buf_slots].reshape(tile_count, key_span, feat_width)
    allowed = jnp.arange(key_span)[None, :] // tile_rows < counts[:, None]

    def head_step(head_idx, carried):
        query_acc, key_acc, value_acc = carried
        col_start = head_idx * HD
        query_head = lax.dynamic_slice_in_dim(query_tiles, col_start, HD, 2)
        key_head = lax.dynamic_slice_in_dim(key_sel, col_start, HD, 2)
        value_head = lax.dynamic_slice_in_dim(value_sel, col_start, HD, 2)
        grad_head = lax.dynamic_slice_in_dim(grad_tiles, col_start, HD, 2)
        scores = (
            jnp.einsum("iqe,ike->iqk", query_head, key_head, preferred_element_type=jnp.float32)
            * score_scale
        )
        scores = jnp.where(allowed[:, None, :], scores, -jnp.inf)
        row_max = jnp.max(scores, axis=-1, keepdims=True)
        log_norm = row_max + jnp.log(jnp.sum(jnp.exp(scores - row_max), axis=-1, keepdims=True))
        weights = jnp.exp(scores - log_norm)
        weights_b = weights.astype(jnp.bfloat16)
        attn_out = jnp.einsum(
            "iqk,ike->iqe", weights_b, value_head, preferred_element_type=jnp.float32
        ).astype(jnp.bfloat16)
        row_delta = jnp.sum(
            grad_head.astype(jnp.float32) * attn_out.astype(jnp.float32), axis=-1, keepdims=True
        )
        dprob = jnp.einsum(
            "iqe,ike->iqk", grad_head, value_head, preferred_element_type=jnp.float32
        )
        dscore = (weights * (dprob - row_delta)).astype(jnp.bfloat16)
        query_head_grad = score_scale * jnp.einsum(
            "iqk,ike->iqe", dscore, key_head, preferred_element_type=jnp.float32
        )
        key_head_grad = score_scale * jnp.einsum(
            "iqk,iqe->ike", dscore, query_head, preferred_element_type=jnp.float32
        )
        value_head_grad = jnp.einsum(
            "iqk,iqe->ike", weights_b, grad_head, preferred_element_type=jnp.float32
        )
        query_acc = lax.dynamic_update_slice_in_dim(query_acc, query_head_grad, col_start, 2)
        key_acc = lax.dynamic_update_slice_in_dim(key_acc, key_head_grad, col_start, 2)
        value_acc = lax.dynamic_update_slice_in_dim(value_acc, value_head_grad, col_start, 2)
        return (query_acc, key_acc, value_acc)

    start_state = (
        jnp.zeros((tile_count, tile_rows, feat_width), jnp.float32),
        jnp.zeros((tile_count, key_span, feat_width), jnp.float32),
        jnp.zeros((tile_count, key_span, feat_width), jnp.float32),
    )
    query_full, key_sel_grad, value_sel_grad = lax.fori_loop(
        0, feat_width // HD, head_step, start_state
    )
    live_slot = jnp.arange(slot_count)[None, :] < counts[:, None]
    routing = (
        (buf_slots[:, :, None] == jnp.arange(buf_tiles)[None, None, :]) & live_slot[:, :, None]
    ).astype(jnp.float32)
    key_grad_buf = jnp.einsum(
        "imb,imr->br",
        routing,
        key_sel_grad.reshape(tile_count, slot_count, tile_rows * feat_width),
        precision=lax.Precision.HIGHEST,
    )
    value_grad_buf = jnp.einsum(
        "imb,imr->br",
        routing,
        value_sel_grad.reshape(tile_count, slot_count, tile_rows * feat_width),
        precision=lax.Precision.HIGHEST,
    )
    return (
        query_full,
        key_grad_buf.reshape(buf_tiles, tile_rows, feat_width),
        value_grad_buf.reshape(buf_tiles, tile_rows, feat_width),
    )


def head_squares(grads_full, head_count):
    rows = grads_full.reshape(-1, head_count, HD)
    return jnp.sum(rows * rows, axis=(0, 2))


def gathered_plan(query_states, key_states, value_states, output_grad, w_out, key_list, key_count):
    seq_count = lax.axis_size("seq")
    seq_index = lax.axis_index("seq")
    tok_rows = query_states.shape[1]
    feat_width = query_states.shape[2]
    head_count = feat_width // HD
    tile_count = tok_rows // TILE
    first_tile = seq_index * tile_count
    own_lists = lax.dynamic_slice_in_dim(key_list[0], first_tile, tile_count, 0)
    own_counts = lax.dynamic_slice_in_dim(key_count[0], first_tile, tile_count, 0)
    grad_out = lax.dot_general(
        lax.all_gather(output_grad, "head", axis=2, tiled=True)[0],
        w_out,
        (((1,), (1,)), ((), ())),
        preferred_element_type=jnp.float32,
    ).astype(jnp.bfloat16)
    query_tiles = query_states[0].reshape(tile_count, TILE, feat_width)
    grad_tiles = grad_out.reshape(tile_count, TILE, feat_width)
    key_whole, value_whole = (
        lax.all_gather(key_states, "seq", axis=1, tiled=True),
        lax.all_gather(value_states, "seq", axis=1, tiled=True),
    )
    key_buf = key_whole[0].reshape(-1, TILE, feat_width)
    value_buf = value_whole[0].reshape(-1, TILE, feat_width)
    query_full, key_grad_buf, value_grad_buf = attend(
        query_tiles, key_buf, value_buf, grad_tiles, own_lists, own_counts
    )
    buf_rows = key_grad_buf.shape[0] * TILE
    key_sum, value_sum = (
        lax.psum_scatter(
            key_grad_buf.reshape(1, buf_rows, feat_width).astype(jnp.bfloat16),
            "seq",
            scatter_dimension=1,
            tiled=True,
        ).astype(jnp.float32),
        lax.psum_scatter(
            value_grad_buf.reshape(1, buf_rows, feat_width).astype(jnp.bfloat16),
            "seq",
            scatter_dimension=1,
            tiled=True,
        ).astype(jnp.float32),
    )
    key_full = key_sum[0]
    value_full = value_sum[0]
    query_rows = query_full.reshape(tok_rows, feat_width)
    local_sums = jnp.stack(
        [
            head_squares(query_rows, head_count),
            head_squares(key_full, head_count),
            head_squares(value_full, head_count),
        ],
        axis=-1,
    )
    total_sums = lax.psum(local_sums, "seq")
    grad_features = jnp.log(total_sums / (seq_count * tok_rows * HD) + 1e-06)
    return (
        query_rows.astype(jnp.bfloat16)[None],
        key_full.astype(jnp.bfloat16)[None],
        value_full.astype(jnp.bfloat16)[None],
        grad_features[None],
    )


MESH_ID = pl.DeviceIdType.MESH
VMEM_BYTES = 58 * 1024 * 1024
NEG_BIG = -1e30
OG_CUTS = 2
F32 = jnp.float32
BF16 = jnp.bfloat16


def dot_nt(a, b):
    return lax.dot_general(a, b, (((1,), (1,)), ((), ())), preferred_element_type=F32)


def dot_nn(a, b):
    return lax.dot_general(a, b, (((1,), (0,)), ((), ())), preferred_element_type=F32)


def fused_kernel(
    n, nh, gc, list_ref, count_ref, q_ref, k_hbm, v_hbm, og_ref, w_hbm,
    dq_ref, dk_ref, dv_ref, feat_ref,
    k_ref, v_ref, w_ref, bias_ref, q_all, g_all, og_all, g_acc, probs, top_ref, inv_ref,
    lse_all, eps_all, part, chain, kt_ref, acc_k, acc_v, acc_q, sq_all,
    guest_out, guest_in, guest_send, guest_recv, back_send, back_recv, load_sem, og_send, og_recv, q_send, q_recv, g_send, g_recv, lse_send, lse_recv,
    eps_send, eps_recv, chain_send, chain_recv, sq_send, sq_recv,
):
    z = lax.axis_index("seq")
    hx = lax.axis_index("head")
    rows, width = q_ref.shape
    heads = width // HD
    feats = og_ref.shape[1]
    key_tiles = rows // TILE
    scale = HD ** (-0.5)
    scale2 = scale * math.log2(math.e)
    has_left = z > 0
    has_right = z < n - 1
    gw = gc * HD
    is_end = (z == 0) | (z == n - 1)
    host_low, host_high = z == 1, z == n - 2
    is_host = (host_low | host_high) if gc else z < 0
    guest = jnp.where(host_low, 0, n - 1)
    host_of = jnp.where(z == 0, 1, n - 2)

    def inner(d):
        return (d > 0) & (d < n - 1)

    def may_go(way, guest_part):
        to = z + (1 - 2 * way)
        return inner(to) if guest_part else (to >= 0) & (to < n)

    loads = [
        pltpu.make_async_copy(src, dst, load_sem.at[i])
        for i, (src, dst) in enumerate(
            ((q_ref, q_all.at[z]), (og_ref, og_all.at[hx]), (w_hbm, w_ref), (k_hbm, k_ref.at[:, 0:width]), (v_hbm, v_ref.at[:, 0:width]))
        )
    ]
    for load in loads:
        load.start()

    def remote(src, dst, ssem, rsem, axis, idx):
        return pltpu.make_async_remote_copy(
            src_ref=src, dst_ref=dst, send_sem=ssem, recv_sem=rsem,
            device_id={axis: idx}, device_id_type=MESH_ID,
        )

    def cols(h):
        return pl.ds(pl.multiple_of(h * HD, HD), HD)

    barrier = pltpu.get_barrier_semaphore()
    for i in range(1, n):
        pl.semaphore_signal(barrier, inc=1, device_id={"seq": lax.rem(z + i, n)}, device_id_type=MESH_ID)
    for i in range(1, nh):
        pl.semaphore_signal(barrier, inc=1, device_id={"head": lax.rem(hx + i, nh)}, device_id_type=MESH_ID)
    pl.semaphore_wait(barrier, n - 1 + nh - 1)

    def og_rows(c):
        return pl.ds(c * (rows // OG_CUTS), rows // OG_CUTS)

    def og_copy(i, c):
        return remote(og_ref.at[og_rows(c)], og_all.at[hx, og_rows(c)], og_send.at[i, c], og_recv.at[hx, c], "head", lax.rem(hx + i, nh))

    def og_arrival(j, c):
        ref = og_all.at[j, og_rows(c)]
        return remote(ref, ref, og_send.at[0, c], og_recv.at[j, c], "head", hx)

    q_parts = [(0, gw), (gw, width - gw)] if gc else [(0, width)]

    def q_own(way, p):
        at = pl.ds(*q_parts[p])
        return remote(q_ref.at[:, at], q_all.at[z, :, at], q_send.at[way, z, p], q_recv.at[z, p], "seq", z + (1 - 2 * way))

    def q_copy(b, way, p):
        ref = q_all.at[b, :, pl.ds(*q_parts[p])]
        return remote(ref, ref, q_send.at[way, b, p], q_recv.at[b, p], "seq", z + (1 - 2 * way))

    def lend(i):
        src, dst = ((k_hbm, k_ref), (v_hbm, v_ref))[i]
        return remote(src.at[:, 0:gw], dst.at[:, width : width + gw], guest_send.at[i], guest_recv.at[i], "seq", host_of)

    def lent(i):
        ref = (k_ref, v_ref)[i].at[:, width : width + gw]
        return remote(ref, ref, guest_send.at[i], guest_recv.at[i], "seq", z)

    def back_copy(h):
        return remote(guest_out.at[h], guest_in.at[h], back_send.at[h], back_recv.at[h], "seq", guest)

    def back_arrival(h):
        return remote(guest_in.at[h], guest_in.at[h], back_send.at[h], back_recv.at[h], "seq", z)

    def g_copy(b, h, way):
        return remote(g_all.at[b, h], g_all.at[b, h], g_send.at[way, b, h], g_recv.at[b, h], "seq", z + (1 - 2 * way))

    def g_own(h, way, c):
        ref = g_all.at[z, h, og_rows(c)]
        return remote(ref, ref, g_send.at[way, z, h], g_recv.at[z, h], "seq", z + (1 - 2 * way))

    def lse_ref(d, p):
        return lse_all.at[d, 0:gc] if p else lse_all.at[d, gc:heads]

    def lse_copy(d, i, p, k):
        return remote(lse_ref(d, p), lse_ref(d, p), lse_send.at[i, k], lse_recv.at[d, p], "seq", lax.rem(z + i, n))

    def lse_arrival(d, p):
        return remote(lse_ref(d, p), lse_ref(d, p), lse_send.at[0, 0], lse_recv.at[d, p], "seq", z)

    def eps_copy(d, h, i, k):
        return remote(eps_all.at[d, h], eps_all.at[d, h], eps_send.at[h, i, k], eps_recv.at[d, h], "seq", lax.rem(z + i, n))

    def eps_arrival(d, h):
        return remote(eps_all.at[d, h], eps_all.at[d, h], eps_send.at[h, 0, 0], eps_recv.at[d, h], "seq", z)

    def lse_sends(act):
        for i in range(1, n):
            act(lse_copy(z, i, 0, 0))
            if gc:
                @pl.when(inner(z) & inner(lax.rem(z + i, n)))
                def _():
                    act(lse_copy(z, i, 1, 1))

                    @pl.when(is_host)
                    def _():
                        act(lse_copy(guest, i, 1, 2))

    def eps_sends(h, act):
        for i in range(1, n):
            @pl.when((h >= gc) | (inner(z) & inner(lax.rem(z + i, n))))
            def _():
                act(eps_copy(z, h, i, 0))

            @pl.when((h < gc) & is_host & inner(lax.rem(z + i, n)))
            def _():
                act(eps_copy(guest, h, i, 1))

    def chain_copy(b, h, way):
        slot = b if way == 0 else jnp.where(b == z - 1, n, b)
        return remote(part.at[b, h], chain.at[slot, h], chain_send.at[b, h], chain_recv.at[slot, h], "seq", z + (1 - 2 * way))

    def chain_arrival(slot, h):
        return remote(chain.at[slot, h], chain.at[slot, h], chain_send.at[0, h], chain_recv.at[slot, h], "seq", z)

    def sq_copy(i):
        return remote(sq_all.at[z], sq_all.at[z], sq_send.at[i], sq_recv.at[z], "seq", lax.rem(z + i, n))

    def sq_arrival(d):
        return remote(sq_all.at[d], sq_all.at[d], sq_send.at[0], sq_recv.at[d], "seq", z)

    def q_own_all(act):
        for p in range(len(q_parts)):
            for way in range(2):
                @pl.when(may_go(way, gc > 0 and p == 0))
                def _():
                    act(q_own(way, p))

    def q_on(s, act):
        for way, b in ((0, z - s), (1, z + s)):
            for p in range(len(q_parts)):
                @pl.when((b >= 0) & (b < n) & may_go(way, gc > 0 and p == 0))
                def _():
                    act(q_copy(b, way, p))

    def g_own_starts(h, c):
        for way in range(2):
            @pl.when(may_go(way, False) & ((h >= gc) | may_go(way, True)))
            def _():
                g_own(h, way, c).start()

    def g_sends(b, h, way, act):
        @pl.when((b >= 0) & (b < n) & may_go(way, False) & ((h >= gc) | may_go(way, True)))
        def _():
            act(g_copy(b, h, way))

    for i in range(1, nh):
        for c in range(OG_CUTS):
            og_copy(i, c).start()
    q_own_all(lambda c: c.start())
    if gc:
        @pl.when(is_end)
        def _():
            lend(0).start()
            lend(1).start()

    tiles, slots = list_ref.shape
    for i in range(tiles):
        for j in range(key_tiles):
            at = (i % key_tiles) * TILE
            for k, owner in enumerate((z, guest) if gc else (z,)):
                bias = jnp.float32(NEG_BIG)
                for m in range(slots):
                    hit = (list_ref[i, m] == owner * key_tiles + j) & (m < count_ref[0, i])
                    bias = jnp.where(hit, jnp.float32(0.0), bias)
                bias_ref[k, i // key_tiles, j, :, at : at + TILE] = jnp.full((1, TILE), bias, F32)

    wide = 256 if width % 256 == 0 else HD

    def features_of(block, j, part_rows, add):
        span = pl.ds(pl.multiple_of(j * feats, HD), feats)

        @pl.loop(0, width // wide)
        def _(c):
            at = pl.ds(pl.multiple_of(c * wide, wide), wide)
            term = dot_nt(block[part_rows, :], w_ref[at, span])
            if add:
                g_acc[c, part_rows, :] = g_acc[c, part_rows, :] + term
            else:
                g_acc[c, part_rows, :] = term

    for load in loads:
        load.wait()
    features_of(og_all.at[hx], hx, slice(0, rows), False)

    def gradient_rows(c):
        part_rows = og_rows(c)
        for i in range(1, nh):
            j = lax.rem(hx + i, nh)
            og_arrival(j, c).wait_recv()
            features_of(og_all.at[j], j, part_rows, True)
        for h in range(heads):
            lo = h * HD
            g_all[z, h, part_rows, :] = g_acc[lo // wide, part_rows, lo % wide : lo % wide + HD].astype(BF16)
            g_own_starts(h, c)

    def q_hop(s):
        for way, b in ((0, z - s), (1, z + s)):
            @pl.when((b >= 0) & (b < n))
            def _():
                for p in range(len(q_parts)):
                    @pl.when(inner(z) if gc > 0 and p == 0 else z >= 0)
                    def _():
                        q_copy(b, way, p).wait_recv()

                        @pl.when(may_go(way, gc > 0 and p == 0))
                        def _():
                            q_copy(b, way, p).start()

    first_head = jnp.where(is_end, gc, 0)

    def softmax_rows(b, low, high):
        @pl.loop(low, high)
        def _(v):
            mine = v < heads
            h = jnp.where(mine, v, v - heads)
            ts = []
            for j in range(key_tiles):
                t = dot_nt(k_ref[j * TILE : (j + 1) * TILE, cols(v)], q_all[b, :, cols(h)])
                ts.append(t * scale2 + bias_ref[jnp.where(mine, 0, 1), b, j])
            top = functools.reduce(jnp.maximum, [jnp.max(t, axis=0, keepdims=True) for t in ts])
            total = jnp.zeros((1, rows), F32)
            for j in range(key_tiles):
                p = jnp.exp2(ts[j] - top)
                total += jnp.sum(p, axis=0, keepdims=True)
                probs[b, v, j * TILE : (j + 1) * TILE, :] = p.astype(BF16)
            top_ref[v, b] = top
            inv_ref[v, b] = 1.0 / total
            lse_all[jnp.where(mine, z, guest), h, b] = top + jnp.log2(total)

    def softmax_at(s):
        @pl.when(z - s >= 0)
        def _():
            softmax_rows(z - s, first_head, heads)

        @pl.when(z + s < n)
        def _():
            softmax_rows(z + s, first_head, heads)

    @pl.loop(0, heads)
    def _(h):
        kt_ref[h] = jnp.transpose(k_ref[:, cols(h)].astype(F32)).astype(BF16)

    softmax_rows(z, first_head, heads)
    for s in range(1, max(n, OG_CUTS + 1)):
        if s < n:
            q_hop(s)
        if s <= OG_CUTS:
            gradient_rows(s - 1)
        if s < n:
            softmax_at(s)
    if gc:
        @pl.when(is_host)
        def _():
            lent(0).wait_recv()
            lent(1).wait_recv()

            @pl.loop(heads, heads + gc)
            def _(v):
                kt_ref[v] = jnp.transpose(k_ref[:, cols(v)].astype(F32)).astype(BF16)

            @pl.loop(0, n)
            def _(b):
                softmax_rows(b, heads, heads + gc)

    lse_sends(lambda c: c.start())

    def g_hop(s, h):
        for way, b in ((0, z - s), (1, z + s)):
            @pl.when((h >= 0) & (h < heads) & (b >= 0) & (b < n) & ((h >= gc) | inner(z)))
            def _():
                g_copy(b, h, way).wait_recv()
                if s < n - 1:
                    g_sends(b, h, way, lambda c: c.start())

    def dprobs(b, v, h, j):
        return dot_nt(v_ref[j * TILE : (j + 1) * TILE, cols(v)], g_all[b, h])

    def holders(h):
        return jnp.where(h < gc, jnp.where(is_end, 0, jnp.where(is_host, 2, 1)), 1)

    def first_pass(h):
        @pl.loop(0, holders(h))
        def _(k):
            v = h + k * heads
            owner = jnp.where(k == 0, z, guest)

            @pl.loop(0, n)
            def _(b):
                eps = jnp.zeros((1, rows), F32)
                for j in range(key_tiles):
                    p = probs[b, v, j * TILE : (j + 1) * TILE, :].astype(F32)
                    eps += jnp.sum(p * dprobs(b, v, h, j), axis=0, keepdims=True)
                eps_all[owner, h, b] = eps * inv_ref[v, b]

        eps_sends(h, lambda c: c.start())

    def second_pass(h):
        for i in range(1, n):
            d = lax.rem(z + i, n)
            skip = (d == guest) & is_host

            @pl.when((h >= gc) | (inner(z) & jnp.logical_not(skip)))
            def _():
                eps_arrival(d, h).wait_recv()

        for b in range(n):
            part[b, h] = jnp.zeros((HD, rows), BF16)

        @pl.loop(0, holders(h))
        def _(k):
            v = h + k * heads
            acc_k[...] = jnp.zeros_like(acc_k)
            acc_v[...] = jnp.zeros_like(acc_v)

            @pl.loop(0, n)
            def _(b):
                logs = [lse_all[d, h, b] for d in range(n)]
                top = functools.reduce(jnp.maximum, logs)
                log_norm = top + jnp.log2(sum(jnp.exp2(x - top) for x in logs))
                delta = sum(jnp.exp2(logs[d] - log_norm) * eps_all[d, h, b] for d in range(n))
                share = jnp.exp2(top_ref[v, b] - log_norm)
                q_b = q_all[b, :, cols(h)]
                g_b = g_all[b, h]
                dq_t = jnp.zeros((HD, rows), F32)
                for j in range(key_tiles):
                    at = slice(j * TILE, (j + 1) * TILE)
                    p = probs[b, v, at, :].astype(F32) * share
                    ds = (p * (dprobs(b, v, h, j) - delta)).astype(BF16)
                    acc_v[at, :] += dot_nn(p.astype(BF16), g_b)
                    acc_k[at, :] += dot_nn(ds, q_b)
                    dq_t += dot_nn(kt_ref[v, :, at], ds)
                part[b, h] = (part[b, h].astype(F32) + dq_t * scale).astype(BF16)

            key_full = acc_k[...] * scale
            value_full = acc_v[...]

            @pl.when(k == 0)
            def _():
                dk_ref[:, cols(h)] = key_full.astype(BF16)
                dv_ref[:, cols(h)] = value_full.astype(BF16)
                sq_all[z, 1, h] = jnp.sum(key_full * key_full, axis=0, keepdims=True)
                sq_all[z, 2, h] = jnp.sum(value_full * value_full, axis=0, keepdims=True)

            if gc:
                @pl.when(k == 1)
                def _():
                    guest_out[h, 0] = key_full.astype(BF16)
                    guest_out[h, 1] = value_full.astype(BF16)
                    back_copy(h).start()

    def take_back(h):
        @pl.when((h >= 0) & (h < gc) & is_end)
        def _():
            back_arrival(h).wait_recv()
            for i, ref in enumerate((dk_ref, dv_ref)):
                ref[:, cols(h)] = guest_in[h, i]
                full = guest_in[h, i].astype(F32)
                sq_all[z, i + 1, h] = jnp.sum(full * full, axis=0, keepdims=True)

    def comes(h, way):
        far = z if way == 0 else n - 1 - z
        return far > jnp.where(h < gc, 1, 0)

    def chain_sends(h, way, act):
        for i in reversed(range(1, n)):
            b = z + i if way == 0 else z - i

            @pl.when((b >= 0) & (b < n) & ((h >= gc) | inner(z)))
            def _():
                act(b)

    def chain_hop(h, way):
        def hop(b):
            @pl.when(comes(h, way))
            def _():
                chain_arrival(b, h).wait_recv()
                part[b, h] = (part[b, h].astype(F32) + chain[b, h].astype(F32)).astype(BF16)

            chain_copy(b, h, way).start()

        @pl.when((h >= 0) & (h < heads))
        def _():
            chain_sends(h, way, hop)

    def own_sum(h):
        @pl.when((h >= 0) & (h < heads))
        def _():
            acc_q[...] = jnp.zeros_like(acc_q)

            @pl.when((h >= gc) | inner(z))
            def _():
                acc_q[...] = part[z, h].astype(F32)

            for way, slot in ((0, z), (1, n)):
                @pl.when(comes(h, way))
                def _():
                    chain_arrival(slot, h).wait_recv()
                    acc_q[...] += chain[slot, h].astype(F32)

            query_full = jnp.transpose(acc_q[...])
            dq_ref[:, cols(h)] = query_full.astype(BF16)
            sq_all[z, 0, h] = jnp.sum(query_full * query_full, axis=0, keepdims=True)

    lead = max(n - 2, 0)

    @pl.loop(0, lead + heads + n)
    def _(step):
        t = step - lead
        for s in range(1, n):
            g_hop(s, t + (n - 1 - s))

        @pl.when((t >= 0) & (t < heads))
        def _():
            first_pass(t)

        @pl.when(t == 1)
        def _():
            for i in range(1, n):
                d = lax.rem(z + i, n)
                lse_arrival(d, 0).wait_recv()
                if gc:
                    skip = (d == guest) & is_host

                    @pl.when(inner(z) & jnp.logical_not(skip))
                    def _():
                        lse_arrival(d, 1).wait_recv()

        @pl.when((t >= 1) & (t <= heads))
        def _():
            second_pass(t - 1)

        chain_hop(t - 1 - z, 0)
        chain_hop(t - 1 - (n - 1 - z), 1)
        own_sum(t - 1 - jnp.maximum(z, n - 1 - z))
        if gc:
            take_back(t - 3)

    for i in range(1, n):
        sq_copy(i).start()
    for i in range(1, n):
        sq_arrival(lax.rem(z + i, n)).wait_recv()
    total = functools.reduce(jnp.add, [sq_all[d] for d in range(n)])
    mean = jnp.sum(total, axis=-1, keepdims=True) / (n * rows * HD)
    logs = jnp.log(mean + 1e-06)
    lane = lax.broadcasted_iota(jnp.int32, (1, HD), 1)
    for j in range(3):
        feat_ref[j] = sum(jnp.where(lane == h, logs[j, h], 0.0) for h in range(heads))

    for i in range(1, nh):
        for c in range(OG_CUTS):
            og_copy(i, c).wait_send()
    for i in range(1, n):
        sq_copy(i).wait_send()
    lse_sends(lambda c: c.wait_send())
    q_own_all(lambda c: c.wait_send())
    for s in range(1, n - 1):
        q_on(s, lambda c: c.wait_send())
    if gc:
        @pl.when(is_end)
        def _():
            lend(0).wait_send()
            lend(1).wait_send()

    @pl.loop(0, heads)
    def _(h):
        for way in range(2):
            for s in range(n - 1):
                b = z - s if way == 0 else z + s

                @pl.when((h >= gc) | inner(z) | (b == z))
                def _():
                    g_sends(b, h, way, lambda c: c.wait_send())

            chain_sends(h, way, lambda b: chain_copy(b, h, way).wait_send())
        eps_sends(h, lambda c: c.wait_send())
        if gc:
            @pl.when((h < gc) & is_host)
            def _():
                back_copy(h).wait_send()


def finish_kernel(dq_in, dk_in, dv_in, feat_in, dq_ref, dk_ref, dv_ref, feat_ref):
    dq_ref[...] = dq_in[...]
    dk_ref[...] = dk_in[...]
    dv_ref[...] = dv_in[...]
    feat_ref[...] = feat_in[:, :, : feat_ref.shape[2]]


def fused_bytes(n, nh, rows, width, feats):
    block = rows * width * 2
    kept = n * (width // HD) * rows * rows * 3
    return block * (5 + 3 * n + n + 1) + rows * feats * 2 * nh + width * feats * nh * 2 + 2 * block + kept


def per_device(query_states, key_states, value_states, output_grad, w_out, key_list, key_count):
    n = lax.axis_size("seq")
    nh = lax.axis_size("head")
    rows, width = query_states.shape[1:]
    feats = output_grad.shape[2]
    if n < 2 or fused_bytes(n, nh, rows, width, feats) > VMEM_BYTES * 3 // 4:
        return gathered_plan(
            query_states, key_states, value_states, output_grad, w_out, key_list, key_count
        )
    heads = width // HD
    key_tiles = rows // TILE
    wide = 256 if width % 256 == 0 else HD
    gc = heads // 3 if n >= 4 else 0
    gn = max(gc, 1)
    vmem = pl.BlockSpec(memory_space=pltpu.VMEM)
    dma = pltpu.SemaphoreType.DMA
    block = jax.ShapeDtypeStruct((rows, width), BF16)
    dq, dk, dv, feat = pl.pallas_call(
        functools.partial(fused_kernel, n, nh, gc),
        out_shape=[block, block, block, jax.ShapeDtypeStruct((3, 1, HD), F32)],
        in_specs=[pl.BlockSpec(memory_space=pltpu.SMEM)] * 2 + [pl.BlockSpec(memory_space=pl.ANY)] * 5,
        out_specs=[vmem] * 4,
        scratch_shapes=[
            pltpu.VMEM((rows, width + gc * HD), BF16),
            pltpu.VMEM((rows, width + gc * HD), BF16),
            pltpu.VMEM((width, feats * nh), BF16),
            pltpu.VMEM((2, n, key_tiles, 1, rows), F32),
            pltpu.VMEM((n, rows, width), BF16),
            pltpu.VMEM((n, heads, rows, HD), BF16),
            pltpu.VMEM((nh, rows, feats), BF16),
            pltpu.VMEM((width // wide, rows, wide), F32),
            pltpu.VMEM((n, heads + gc, rows, rows), BF16),
            pltpu.VMEM((heads + gc, n, 1, rows), F32),
            pltpu.VMEM((heads + gc, n, 1, rows), F32),
            pltpu.VMEM((n, heads, n, 1, rows), F32),
            pltpu.VMEM((n, heads, n, 1, rows), F32),
            pltpu.VMEM((n, heads, HD, rows), BF16),
            pltpu.VMEM((n + 1, heads, HD, rows), BF16),
            pltpu.VMEM((heads + gc, HD, rows), BF16),
            pltpu.VMEM((rows, HD), F32),
            pltpu.VMEM((rows, HD), F32),
            pltpu.VMEM((HD, rows), F32),
            pltpu.VMEM((n, 3, heads, 1, HD), F32),
            pltpu.VMEM((gn, 2, rows, HD), BF16),
            pltpu.VMEM((gn, 2, rows, HD), BF16),
            dma((2,)), dma((2,)), dma((gn,)), dma((gn,)),
            dma((5,)),
            dma((nh, OG_CUTS)), dma((nh, OG_CUTS)),
            dma((2, n, 2)), dma((n, 2)),
            dma((2, n, heads)), dma((n, heads)),
            dma((n, 3)), dma((n, 2)),
            dma((heads, n, 2)), dma((n, heads)),
            dma((n, heads)), dma((n + 1, heads)),
            dma((n,)), dma((n,)),
        ],
        compiler_params=pltpu.CompilerParams(
            collective_id=0, has_side_effects=True, vmem_limit_bytes=VMEM_BYTES
        ),
        cost_estimate=pl.CostEstimate(
            flops=14 * rows * rows * n * width + 2 * rows * width * feats * nh,
            bytes_accessed=16 * rows * width,
            transcendentals=2 * rows * rows * n * heads,
        ),
    )(key_list[0], key_count, query_states[0], key_states[0], value_states[0], output_grad[0], w_out)
    dq, dk, dv, grad_features = pl.pallas_call(
        finish_kernel,
        out_shape=[block, block, block, jax.ShapeDtypeStruct((3, 1, heads), F32)],
        in_specs=[vmem] * 4,
        out_specs=[vmem] * 4,
    )(dq, dk, dv, feat)
    return dq[None], dk[None], dv[None], jnp.transpose(grad_features, (1, 2, 0))


def solution(mesh):
    in_specs = (
        P(("grp", "clip"), "seq", "head"),
        P(("grp", "clip"), "seq", "head"),
        P(("grp", "clip"), "seq", "head"),
        P(("grp", "clip"), "seq", "head"),
        P("head", None),
        P(("grp", "clip"), None, None),
        P(("grp", "clip"), None),
    )
    out_specs = (
        P(("grp", "clip"), "seq", "head"),
        P(("grp", "clip"), "seq", "head"),
        P(("grp", "clip"), "seq", "head"),
        P(("grp", "clip"), "head", None),
    )
    return jax.shard_map(
        per_device, mesh=mesh, in_specs=in_specs, out_specs=out_specs, check_vma=False
    )
```

```python
import functools
import math

import jax
import jax.numpy as jnp
from jax import lax
from jax.experimental import pallas as pl
from jax.experimental.pallas import tpu as pltpu
from jax.sharding import PartitionSpec as P

HD = 128
TILE = 256


def attend(query_tiles, key_buf, value_buf, grad_tiles, buf_slots, counts):
    score_scale = HD ** (-0.5)
    tile_count, tile_rows, feat_width = query_tiles.shape
    slot_count = buf_slots.shape[1]
    key_span = slot_count * tile_rows
    buf_tiles = key_buf.shape[0]
    key_sel = key_buf[buf_slots].reshape(tile_count, key_span, feat_width)
    value_sel = value_buf[buf_slots].reshape(tile_count, key_span, feat_width)
    allowed = jnp.arange(key_span)[None, :] // tile_rows < counts[:, None]

    def head_step(head_idx, carried):
        query_acc, key_acc, value_acc = carried
        col_start = head_idx * HD
        query_head = lax.dynamic_slice_in_dim(query_tiles, col_start, HD, 2)
        key_head = lax.dynamic_slice_in_dim(key_sel, col_start, HD, 2)
        value_head = lax.dynamic_slice_in_dim(value_sel, col_start, HD, 2)
        grad_head = lax.dynamic_slice_in_dim(grad_tiles, col_start, HD, 2)
        scores = (
            jnp.einsum("iqe,ike->iqk", query_head, key_head, preferred_element_type=jnp.float32)
            * score_scale
        )
        scores = jnp.where(allowed[:, None, :], scores, -jnp.inf)
        row_max = jnp.max(scores, axis=-1, keepdims=True)
        log_norm = row_max + jnp.log(jnp.sum(jnp.exp(scores - row_max), axis=-1, keepdims=True))
        weights = jnp.exp(scores - log_norm)
        weights_b = weights.astype(jnp.bfloat16)
        attn_out = jnp.einsum(
            "iqk,ike->iqe", weights_b, value_head, preferred_element_type=jnp.float32
        ).astype(jnp.bfloat16)
        row_delta = jnp.sum(
            grad_head.astype(jnp.float32) * attn_out.astype(jnp.float32), axis=-1, keepdims=True
        )
        dprob = jnp.einsum(
            "iqe,ike->iqk", grad_head, value_head, preferred_element_type=jnp.float32
        )
        dscore = (weights * (dprob - row_delta)).astype(jnp.bfloat16)
        query_head_grad = score_scale * jnp.einsum(
            "iqk,ike->iqe", dscore, key_head, preferred_element_type=jnp.float32
        )
        key_head_grad = score_scale * jnp.einsum(
            "iqk,iqe->ike", dscore, query_head, preferred_element_type=jnp.float32
        )
        value_head_grad = jnp.einsum(
            "iqk,iqe->ike", weights_b, grad_head, preferred_element_type=jnp.float32
        )
        query_acc = lax.dynamic_update_slice_in_dim(query_acc, query_head_grad, col_start, 2)
        key_acc = lax.dynamic_update_slice_in_dim(key_acc, key_head_grad, col_start, 2)
        value_acc = lax.dynamic_update_slice_in_dim(value_acc, value_head_grad, col_start, 2)
        return (query_acc, key_acc, value_acc)

    start_state = (
        jnp.zeros((tile_count, tile_rows, feat_width), jnp.float32),
        jnp.zeros((tile_count, key_span, feat_width), jnp.float32),
        jnp.zeros((tile_count, key_span, feat_width), jnp.float32),
    )
    query_full, key_sel_grad, value_sel_grad = lax.fori_loop(
        0, feat_width // HD, head_step, start_state
    )
    live_slot = jnp.arange(slot_count)[None, :] < counts[:, None]
    routing = (
        (buf_slots[:, :, None] == jnp.arange(buf_tiles)[None, None, :]) & live_slot[:, :, None]
    ).astype(jnp.float32)
    key_grad_buf = jnp.einsum(
        "imb,imr->br",
        routing,
        key_sel_grad.reshape(tile_count, slot_count, tile_rows * feat_width),
        precision=lax.Precision.HIGHEST,
    )
    value_grad_buf = jnp.einsum(
        "imb,imr->br",
        routing,
        value_sel_grad.reshape(tile_count, slot_count, tile_rows * feat_width),
        precision=lax.Precision.HIGHEST,
    )
    return (
        query_full,
        key_grad_buf.reshape(buf_tiles, tile_rows, feat_width),
        value_grad_buf.reshape(buf_tiles, tile_rows, feat_width),
    )


def head_squares(grads_full, head_count):
    rows = grads_full.reshape(-1, head_count, HD)
    return jnp.sum(rows * rows, axis=(0, 2))


def gathered_plan(query_states, key_states, value_states, output_grad, w_out, key_list, key_count):
    seq_count = lax.axis_size("seq")
    seq_index = lax.axis_index("seq")
    tok_rows = query_states.shape[1]
    feat_width = query_states.shape[2]
    head_count = feat_width // HD
    tile_count = tok_rows // TILE
    first_tile = seq_index * tile_count
    own_lists = lax.dynamic_slice_in_dim(key_list[0], first_tile, tile_count, 0)
    own_counts = lax.dynamic_slice_in_dim(key_count[0], first_tile, tile_count, 0)
    grad_out = lax.dot_general(
        lax.all_gather(output_grad, "head", axis=2, tiled=True)[0],
        w_out,
        (((1,), (1,)), ((), ())),
        preferred_element_type=jnp.float32,
    ).astype(jnp.bfloat16)
    query_tiles = query_states[0].reshape(tile_count, TILE, feat_width)
    grad_tiles = grad_out.reshape(tile_count, TILE, feat_width)
    key_whole, value_whole = (
        lax.all_gather(key_states, "seq", axis=1, tiled=True),
        lax.all_gather(value_states, "seq", axis=1, tiled=True),
    )
    key_buf = key_whole[0].reshape(-1, TILE, feat_width)
    value_buf = value_whole[0].reshape(-1, TILE, feat_width)
    query_full, key_grad_buf, value_grad_buf = attend(
        query_tiles, key_buf, value_buf, grad_tiles, own_lists, own_counts
    )
    buf_rows = key_grad_buf.shape[0] * TILE
    key_sum, value_sum = (
        lax.psum_scatter(
            key_grad_buf.reshape(1, buf_rows, feat_width).astype(jnp.bfloat16),
            "seq",
            scatter_dimension=1,
            tiled=True,
        ).astype(jnp.float32),
        lax.psum_scatter(
            value_grad_buf.reshape(1, buf_rows, feat_width).astype(jnp.bfloat16),
            "seq",
            scatter_dimension=1,
            tiled=True,
        ).astype(jnp.float32),
    )
    key_full = key_sum[0]
    value_full = value_sum[0]
    query_rows = query_full.reshape(tok_rows, feat_width)
    local_sums = jnp.stack(
        [
            head_squares(query_rows, head_count),
            head_squares(key_full, head_count),
            head_squares(value_full, head_count),
        ],
        axis=-1,
    )
    total_sums = lax.psum(local_sums, "seq")
    grad_features = jnp.log(total_sums / (seq_count * tok_rows * HD) + 1e-06)
    return (
        query_rows.astype(jnp.bfloat16)[None],
        key_full.astype(jnp.bfloat16)[None],
        value_full.astype(jnp.bfloat16)[None],
        grad_features[None],
    )


MESH_ID = pl.DeviceIdType.MESH
VMEM_BYTES = 58 * 1024 * 1024
NEG_BIG = -1e30
OG_CUTS = 2
AHEAD = 1
F32 = jnp.float32
BF16 = jnp.bfloat16


def dot_nt(a, b):
    return lax.dot_general(a, b, (((1,), (1,)), ((), ())), preferred_element_type=F32)


def dot_nn(a, b):
    return lax.dot_general(a, b, (((1,), (0,)), ((), ())), preferred_element_type=F32)


def fused_kernel(
    n, nh, gc, list_ref, count_ref, q_ref, k_hbm, v_hbm, og_ref, w_hbm,
    dq_ref, dk_ref, dv_ref, feat_ref,
    k_ref, v_ref, w_ref, bias_ref, q_all, g_all, og_all, g_acc, probs, top_ref, inv_ref,
    lse_all, eps_all, part, chain, kt_ref, acc_k, acc_v, acc_q, sq_all,
    guest_out, guest_in, guest_send, guest_recv, back_send, back_recv, load_sem, og_send, og_recv, q_send, q_recv, g_send, g_recv, lse_send, lse_recv,
    eps_send, eps_recv, chain_send, chain_recv, sq_send, sq_recv,
):
    z = lax.axis_index("seq")
    hx = lax.axis_index("head")
    rows, width = q_ref.shape
    heads = width // HD
    feats = og_ref.shape[1]
    key_tiles = rows // TILE
    scale = HD ** (-0.5)
    scale2 = scale * math.log2(math.e)
    has_left = z > 0
    has_right = z < n - 1
    gw = gc * HD
    is_end = (z == 0) | (z == n - 1)
    host_low, host_high = z == 1, z == n - 2
    is_host = (host_low | host_high) if gc else z < 0
    guest = jnp.where(host_low, 0, n - 1)
    host_of = jnp.where(z == 0, 1, n - 2)

    def inner(d):
        return (d > 0) & (d < n - 1)

    def may_go(way, guest_part):
        to = z + (1 - 2 * way)
        return inner(to) if guest_part else (to >= 0) & (to < n)

    loads = [
        pltpu.make_async_copy(src, dst, load_sem.at[i])
        for i, (src, dst) in enumerate(
            ((q_ref, q_all.at[z]), (og_ref, og_all.at[hx]), (w_hbm, w_ref), (k_hbm, k_ref.at[:, 0:width]), (v_hbm, v_ref.at[:, 0:width]))
        )
    ]
    for load in loads:
        load.start()

    def remote(src, dst, ssem, rsem, axis, idx):
        return pltpu.make_async_remote_copy(
            src_ref=src, dst_ref=dst, send_sem=ssem, recv_sem=rsem,
            device_id={axis: idx}, device_id_type=MESH_ID,
        )

    def cols(h):
        return pl.ds(pl.multiple_of(h * HD, HD), HD)

    barrier = pltpu.get_barrier_semaphore()
    for i in range(1, n):
        pl.semaphore_signal(barrier, inc=1, device_id={"seq": lax.rem(z + i, n)}, device_id_type=MESH_ID)
    for i in range(1, nh):
        pl.semaphore_signal(barrier, inc=1, device_id={"head": lax.rem(hx + i, nh)}, device_id_type=MESH_ID)
    pl.semaphore_wait(barrier, n - 1 + nh - 1)

    def og_rows(c):
        return pl.ds(c * (rows // OG_CUTS), rows // OG_CUTS)

    def og_copy(i, c):
        return remote(og_ref.at[og_rows(c)], og_all.at[hx, og_rows(c)], og_send.at[i, c], og_recv.at[hx, c], "head", lax.rem(hx + i, nh))

    def og_arrival(j, c):
        ref = og_all.at[j, og_rows(c)]
        return remote(ref, ref, og_send.at[0, c], og_recv.at[j, c], "head", hx)

    q_parts = [(0, gw), (gw, width - gw)] if gc else [(0, width)]

    def q_own(way, p):
        at = pl.ds(*q_parts[p])
        return remote(q_ref.at[:, at], q_all.at[z, :, at], q_send.at[way, z, p], q_recv.at[z, p], "seq", z + (1 - 2 * way))

    def q_copy(b, way, p):
        ref = q_all.at[b, :, pl.ds(*q_parts[p])]
        return remote(ref, ref, q_send.at[way, b, p], q_recv.at[b, p], "seq", z + (1 - 2 * way))

    def lend(i):
        src, dst = ((k_hbm, k_ref), (v_hbm, v_ref))[i]
        return remote(src.at[:, 0:gw], dst.at[:, width : width + gw], guest_send.at[i], guest_recv.at[i], "seq", host_of)

    def lent(i):
        ref = (k_ref, v_ref)[i].at[:, width : width + gw]
        return remote(ref, ref, guest_send.at[i], guest_recv.at[i], "seq", z)

    def back_copy(h):
        return remote(guest_out.at[h], guest_in.at[h], back_send.at[h], back_recv.at[h], "seq", guest)

    def back_arrival(h):
        return remote(guest_in.at[h], guest_in.at[h], back_send.at[h], back_recv.at[h], "seq", z)

    def g_copy(b, h, way):
        return remote(g_all.at[b, h], g_all.at[b, h], g_send.at[way, b, h], g_recv.at[b, h], "seq", z + (1 - 2 * way))

    def g_own(h, way, c):
        ref = g_all.at[z, h, og_rows(c)]
        return remote(ref, ref, g_send.at[way, z, h], g_recv.at[z, h], "seq", z + (1 - 2 * way))

    def lse_ref(d, p):
        return lse_all.at[d, 0:gc] if p else lse_all.at[d, gc:heads]

    def lse_copy(d, i, p, k):
        return remote(lse_ref(d, p), lse_ref(d, p), lse_send.at[i, k], lse_recv.at[d, p], "seq", lax.rem(z + i, n))

    def lse_arrival(d, p):
        return remote(lse_ref(d, p), lse_ref(d, p), lse_send.at[0, 0], lse_recv.at[d, p], "seq", z)

    def eps_copy(d, h, i, k):
        return remote(eps_all.at[d, h], eps_all.at[d, h], eps_send.at[h, i, k], eps_recv.at[d, h], "seq", lax.rem(z + i, n))

    def eps_arrival(d, h):
        return remote(eps_all.at[d, h], eps_all.at[d, h], eps_send.at[h, 0, 0], eps_recv.at[d, h], "seq", z)

    def lse_sends(act):
        for i in range(1, n):
            act(lse_copy(z, i, 0, 0))
            if gc:
                @pl.when(inner(z) & inner(lax.rem(z + i, n)))
                def _():
                    act(lse_copy(z, i, 1, 1))

                    @pl.when(is_host)
                    def _():
                        act(lse_copy(guest, i, 1, 2))

    def eps_sends(h, act):
        for i in range(1, n):
            @pl.when((h >= gc) | (inner(z) & inner(lax.rem(z + i, n))))
            def _():
                act(eps_copy(z, h, i, 0))

            @pl.when((h < gc) & is_host & inner(lax.rem(z + i, n)))
            def _():
                act(eps_copy(guest, h, i, 1))

    def chain_copy(b, h, way):
        slot = b if way == 0 else jnp.where(b == z - 1, n, b)
        return remote(part.at[b, h], chain.at[slot, h], chain_send.at[b, h], chain_recv.at[slot, h], "seq", z + (1 - 2 * way))

    def chain_arrival(slot, h):
        return remote(chain.at[slot, h], chain.at[slot, h], chain_send.at[0, h], chain_recv.at[slot, h], "seq", z)

    def sq_copy(i):
        return remote(sq_all.at[z], sq_all.at[z], sq_send.at[i], sq_recv.at[z], "seq", lax.rem(z + i, n))

    def sq_arrival(d):
        return remote(sq_all.at[d], sq_all.at[d], sq_send.at[0], sq_recv.at[d], "seq", z)

    def q_own_all(act):
        for p in range(len(q_parts)):
            for way in range(2):
                @pl.when(may_go(way, gc > 0 and p == 0))
                def _():
                    act(q_own(way, p))

    def q_on(s, act):
        for way, b in ((0, z - s), (1, z + s)):
            for p in range(len(q_parts)):
                @pl.when((b >= 0) & (b < n) & may_go(way, gc > 0 and p == 0))
                def _():
                    act(q_copy(b, way, p))

    def g_own_starts(h, c):
        for way in range(2):
            @pl.when(may_go(way, False) & ((h >= gc) | may_go(way, True)))
            def _():
                g_own(h, way, c).start()

    def g_sends(b, h, way, act):
        @pl.when((b >= 0) & (b < n) & may_go(way, False) & ((h >= gc) | may_go(way, True)))
        def _():
            act(g_copy(b, h, way))

    for i in range(1, nh):
        for c in range(OG_CUTS):
            og_copy(i, c).start()
    q_own_all(lambda c: c.start())
    if gc:
        @pl.when(is_end)
        def _():
            lend(0).start()
            lend(1).start()

    tiles, slots = list_ref.shape
    for i in range(tiles):
        for j in range(key_tiles):
            at = (i % key_tiles) * TILE
            for k, owner in enumerate((z, guest) if gc else (z,)):
                bias = jnp.float32(NEG_BIG)
                for m in range(slots):
                    hit = (list_ref[i, m] == owner * key_tiles + j) & (m < count_ref[0, i])
                    bias = jnp.where(hit, jnp.float32(0.0), bias)
                bias_ref[k, i // key_tiles, j, :, at : at + TILE] = jnp.full((1, TILE), bias, F32)

    wide = 256 if width % 256 == 0 else HD

    def features_of(block, j, part_rows, add):
        span = pl.ds(pl.multiple_of(j * feats, HD), feats)

        @pl.loop(0, width // wide)
        def _(c):
            at = pl.ds(pl.multiple_of(c * wide, wide), wide)
            term = dot_nt(block[part_rows, :], w_ref[at, span])
            if add:
                g_acc[c, part_rows, :] = g_acc[c, part_rows, :] + term
            else:
                g_acc[c, part_rows, :] = term

    for load in loads:
        load.wait()
    features_of(og_all.at[hx], hx, slice(0, rows), False)

    def gradient_rows(c):
        part_rows = og_rows(c)
        for i in range(1, nh):
            j = lax.rem(hx + i, nh)
            og_arrival(j, c).wait_recv()
            features_of(og_all.at[j], j, part_rows, True)
        for h in range(heads):
            lo = h * HD
            g_all[z, h, part_rows, :] = g_acc[lo // wide, part_rows, lo % wide : lo % wide + HD].astype(BF16)
            g_own_starts(h, c)

    def q_hop(s):
        for way, b in ((0, z - s), (1, z + s)):
            @pl.when((b >= 0) & (b < n))
            def _():
                for p in range(len(q_parts)):
                    @pl.when(inner(z) if gc > 0 and p == 0 else z >= 0)
                    def _():
                        q_copy(b, way, p).wait_recv()

                        @pl.when(may_go(way, gc > 0 and p == 0))
                        def _():
                            q_copy(b, way, p).start()

    first_head = jnp.where(is_end, gc, 0)

    def softmax_rows(b, low, high):
        @pl.loop(low, high)
        def _(v):
            mine = v < heads
            h = jnp.where(mine, v, v - heads)
            ts = []
            for j in range(key_tiles):
                t = dot_nt(k_ref[j * TILE : (j + 1) * TILE, cols(v)], q_all[b, :, cols(h)])
                ts.append(t * scale2 + bias_ref[jnp.where(mine, 0, 1), b, j])
            top = functools.reduce(jnp.maximum, [jnp.max(t, axis=0, keepdims=True) for t in ts])
            total = jnp.zeros((1, rows), F32)
            for j in range(key_tiles):
                p = jnp.exp2(ts[j] - top)
                total += jnp.sum(p, axis=0, keepdims=True)
                probs[b, v, j * TILE : (j + 1) * TILE, :] = p.astype(BF16)
            top_ref[v, b] = top
            inv_ref[v, b] = 1.0 / total
            lse_all[jnp.where(mine, z, guest), h, b] = top + jnp.log2(total)

    def softmax_at(s):
        @pl.when(z - s >= 0)
        def _():
            softmax_rows(z - s, first_head, heads)

        @pl.when(z + s < n)
        def _():
            softmax_rows(z + s, first_head, heads)

    @pl.loop(0, heads)
    def _(h):
        kt_ref[h] = jnp.transpose(k_ref[:, cols(h)].astype(F32)).astype(BF16)

    softmax_rows(z, first_head, heads)
    for s in range(1, max(n, OG_CUTS + 1)):
        if s < n:
            q_hop(s)
        if s <= OG_CUTS:
            gradient_rows(s - 1)
        if s < n:
            softmax_at(s)
    def g_hop(s, h):
        for way, b in ((0, z - s), (1, z + s)):
            @pl.when((h >= 0) & (h < heads) & (b >= 0) & (b < n) & ((h >= gc) | inner(z)))
            def _():
                g_copy(b, h, way).wait_recv()
                if s < n - 1:
                    g_sends(b, h, way, lambda c: c.start())

    def g_hops(t):
        for s in range(1, n):
            g_hop(s, t + (n - 1 - s) + AHEAD)

    lead = n - 2 + AHEAD

    @pl.loop(0, lead)
    def _(step):
        g_hops(step - lead)

    if gc:
        @pl.when(is_host)
        def _():
            lent(0).wait_recv()
            lent(1).wait_recv()

            @pl.loop(heads, heads + gc)
            def _(v):
                kt_ref[v] = jnp.transpose(k_ref[:, cols(v)].astype(F32)).astype(BF16)

            @pl.loop(0, n)
            def _(b):
                softmax_rows(b, heads, heads + gc)

    lse_sends(lambda c: c.start())

    def dprobs(b, v, h, j):
        return dot_nt(v_ref[j * TILE : (j + 1) * TILE, cols(v)], g_all[b, h])

    def holders(h):
        return jnp.where(h < gc, jnp.where(is_end, 0, jnp.where(is_host, 2, 1)), 1)

    def first_pass(h):
        @pl.loop(0, holders(h))
        def _(k):
            v = h + k * heads
            owner = jnp.where(k == 0, z, guest)

            @pl.loop(0, n)
            def _(b):
                eps = jnp.zeros((1, rows), F32)
                for j in range(key_tiles):
                    p = probs[b, v, j * TILE : (j + 1) * TILE, :].astype(F32)
                    eps += jnp.sum(p * dprobs(b, v, h, j), axis=0, keepdims=True)
                eps_all[owner, h, b] = eps * inv_ref[v, b]

        eps_sends(h, lambda c: c.start())

    def second_pass(h):
        for i in range(1, n):
            d = lax.rem(z + i, n)
            skip = (d == guest) & is_host

            @pl.when((h >= gc) | (inner(z) & jnp.logical_not(skip)))
            def _():
                eps_arrival(d, h).wait_recv()

        for b in range(n):
            part[b, h] = jnp.zeros((HD, rows), BF16)

        @pl.loop(0, holders(h))
        def _(k):
            v = h + k * heads
            acc_k[...] = jnp.zeros_like(acc_k)
            acc_v[...] = jnp.zeros_like(acc_v)

            @pl.loop(0, n)
            def _(b):
                logs = [lse_all[d, h, b] for d in range(n)]
                top = functools.reduce(jnp.maximum, logs)
                log_norm = top + jnp.log2(sum(jnp.exp2(x - top) for x in logs))
                delta = sum(jnp.exp2(logs[d] - log_norm) * eps_all[d, h, b] for d in range(n))
                share = jnp.exp2(top_ref[v, b] - log_norm)
                q_b = q_all[b, :, cols(h)]
                g_b = g_all[b, h]
                dq_t = jnp.zeros((HD, rows), F32)
                for j in range(key_tiles):
                    at = slice(j * TILE, (j + 1) * TILE)
                    p = probs[b, v, at, :].astype(F32) * share
                    ds = (p * (dprobs(b, v, h, j) - delta)).astype(BF16)
                    acc_v[at, :] += dot_nn(p.astype(BF16), g_b)
                    acc_k[at, :] += dot_nn(ds, q_b)
                    dq_t += dot_nn(kt_ref[v, :, at], ds)
                part[b, h] = (part[b, h].astype(F32) + dq_t * scale).astype(BF16)

            key_full = acc_k[...] * scale
            value_full = acc_v[...]

            @pl.when(k == 0)
            def _():
                dk_ref[:, cols(h)] = key_full.astype(BF16)
                dv_ref[:, cols(h)] = value_full.astype(BF16)
                sq_all[z, 1, h] = jnp.sum(key_full * key_full, axis=0, keepdims=True)
                sq_all[z, 2, h] = jnp.sum(value_full * value_full, axis=0, keepdims=True)

            if gc:
                @pl.when(k == 1)
                def _():
                    guest_out[h, 0] = key_full.astype(BF16)
                    guest_out[h, 1] = value_full.astype(BF16)
                    back_copy(h).start()

    def take_back(h):
        @pl.when((h >= 0) & (h < gc) & is_end)
        def _():
            back_arrival(h).wait_recv()
            for i, ref in enumerate((dk_ref, dv_ref)):
                ref[:, cols(h)] = guest_in[h, i]
                full = guest_in[h, i].astype(F32)
                sq_all[z, i + 1, h] = jnp.sum(full * full, axis=0, keepdims=True)

    def comes(h, way):
        far = z if way == 0 else n - 1 - z
        return far > jnp.where(h < gc, 1, 0)

    def chain_sends(h, way, act):
        for i in reversed(range(1, n)):
            b = z + i if way == 0 else z - i

            @pl.when((b >= 0) & (b < n) & ((h >= gc) | inner(z)))
            def _():
                act(b)

    def chain_hop(h, way):
        def hop(b):
            @pl.when(comes(h, way))
            def _():
                chain_arrival(b, h).wait_recv()
                part[b, h] = (part[b, h].astype(F32) + chain[b, h].astype(F32)).astype(BF16)

            chain_copy(b, h, way).start()

        @pl.when((h >= 0) & (h < heads))
        def _():
            chain_sends(h, way, hop)

    def own_sum(h):
        @pl.when((h >= 0) & (h < heads))
        def _():
            acc_q[...] = jnp.zeros_like(acc_q)

            @pl.when((h >= gc) | inner(z))
            def _():
                acc_q[...] = part[z, h].astype(F32)

            for way, slot in ((0, z), (1, n)):
                @pl.when(comes(h, way))
                def _():
                    chain_arrival(slot, h).wait_recv()
                    acc_q[...] += chain[slot, h].astype(F32)

            query_full = jnp.transpose(acc_q[...])
            dq_ref[:, cols(h)] = query_full.astype(BF16)
            sq_all[z, 0, h] = jnp.sum(query_full * query_full, axis=0, keepdims=True)

    @pl.loop(0, heads + n)
    def _(t):
        g_hops(t)

        @pl.when((t >= 0) & (t < heads))
        def _():
            first_pass(t)

        @pl.when(t == 1)
        def _():
            for i in range(1, n):
                d = lax.rem(z + i, n)
                lse_arrival(d, 0).wait_recv()
                if gc:
                    skip = (d == guest) & is_host

                    @pl.when(inner(z) & jnp.logical_not(skip))
                    def _():
                        lse_arrival(d, 1).wait_recv()

        @pl.when((t >= 1) & (t <= heads))
        def _():
            second_pass(t - 1)

        chain_hop(t - 1 - z, 0)
        chain_hop(t - 1 - (n - 1 - z), 1)
        own_sum(t - 1 - jnp.maximum(z, n - 1 - z))
        if gc:
            take_back(t - 3)

    for i in range(1, n):
        sq_copy(i).start()
    for i in range(1, n):
        sq_arrival(lax.rem(z + i, n)).wait_recv()
    total = functools.reduce(jnp.add, [sq_all[d] for d in range(n)])
    mean = jnp.sum(total, axis=-1, keepdims=True) / (n * rows * HD)
    logs = jnp.log(mean + 1e-06)
    lane = lax.broadcasted_iota(jnp.int32, (1, HD), 1)
    for j in range(3):
        feat_ref[j] = sum(jnp.where(lane == h, logs[j, h], 0.0) for h in range(heads))

    for i in range(1, nh):
        for c in range(OG_CUTS):
            og_copy(i, c).wait_send()
    for i in range(1, n):
        sq_copy(i).wait_send()
    lse_sends(lambda c: c.wait_send())
    q_own_all(lambda c: c.wait_send())
    for s in range(1, n - 1):
        q_on(s, lambda c: c.wait_send())
    if gc:
        @pl.when(is_end)
        def _():
            lend(0).wait_send()
            lend(1).wait_send()

    @pl.loop(0, heads)
    def _(h):
        for way in range(2):
            for s in range(n - 1):
                b = z - s if way == 0 else z + s

                @pl.when((h >= gc) | inner(z) | (b == z))
                def _():
                    g_sends(b, h, way, lambda c: c.wait_send())

            chain_sends(h, way, lambda b: chain_copy(b, h, way).wait_send())
        eps_sends(h, lambda c: c.wait_send())
        if gc:
            @pl.when((h < gc) & is_host)
            def _():
                back_copy(h).wait_send()


def finish_kernel(dq_in, dk_in, dv_in, feat_in, dq_ref, dk_ref, dv_ref, feat_ref):
    dq_ref[...] = dq_in[...]
    dk_ref[...] = dk_in[...]
    dv_ref[...] = dv_in[...]
    feat_ref[...] = feat_in[:, :, : feat_ref.shape[2]]


def fused_bytes(n, nh, rows, width, feats):
    block = rows * width * 2
    kept = n * (width // HD) * rows * rows * 3
    return block * (5 + 3 * n + n + 1) + rows * feats * 2 * nh + width * feats * nh * 2 + 2 * block + kept


def per_device(query_states, key_states, value_states, output_grad, w_out, key_list, key_count):
    n = lax.axis_size("seq")
    nh = lax.axis_size("head")
    rows, width = query_states.shape[1:]
    feats = output_grad.shape[2]
    if n < 2 or fused_bytes(n, nh, rows, width, feats) > VMEM_BYTES * 3 // 4:
        return gathered_plan(
            query_states, key_states, value_states, output_grad, w_out, key_list, key_count
        )
    heads = width // HD
    key_tiles = rows // TILE
    wide = 256 if width % 256 == 0 else HD
    gc = 2 * heads // 3 if n >= 4 else 0
    gn = max(gc, 1)
    vmem = pl.BlockSpec(memory_space=pltpu.VMEM)
    dma = pltpu.SemaphoreType.DMA
    block = jax.ShapeDtypeStruct((rows, width), BF16)
    dq, dk, dv, feat = pl.pallas_call(
        functools.partial(fused_kernel, n, nh, gc),
        out_shape=[block, block, block, jax.ShapeDtypeStruct((3, 1, HD), F32)],
        in_specs=[pl.BlockSpec(memory_space=pltpu.SMEM)] * 2 + [pl.BlockSpec(memory_space=pl.ANY)] * 5,
        out_specs=[vmem] * 4,
        scratch_shapes=[
            pltpu.VMEM((rows, width + gc * HD), BF16),
            pltpu.VMEM((rows, width + gc * HD), BF16),
            pltpu.VMEM((width, feats * nh), BF16),
            pltpu.VMEM((2, n, key_tiles, 1, rows), F32),
            pltpu.VMEM((n, rows, width), BF16),
            pltpu.VMEM((n, heads, rows, HD), BF16),
            pltpu.VMEM((nh, rows, feats), BF16),
            pltpu.VMEM((width // wide, rows, wide), F32),
            pltpu.VMEM((n, heads + gc, rows, rows), BF16),
            pltpu.VMEM((heads + gc, n, 1, rows), F32),
            pltpu.VMEM((heads + gc, n, 1, rows), F32),
            pltpu.VMEM((n, heads, n, 1, rows), F32),
            pltpu.VMEM((n, heads, n, 1, rows), F32),
            pltpu.VMEM((n, heads, HD, rows), BF16),
            pltpu.VMEM((n + 1, heads, HD, rows), BF16),
            pltpu.VMEM((heads + gc, HD, rows), BF16),
            pltpu.VMEM((rows, HD), F32),
            pltpu.VMEM((rows, HD), F32),
            pltpu.VMEM((HD, rows), F32),
            pltpu.VMEM((n, 3, heads, 1, HD), F32),
            pltpu.VMEM((gn, 2, rows, HD), BF16),
            pltpu.VMEM((gn, 2, rows, HD), BF16),
            dma((2,)), dma((2,)), dma((gn,)), dma((gn,)),
            dma((5,)),
            dma((nh, OG_CUTS)), dma((nh, OG_CUTS)),
            dma((2, n, 2)), dma((n, 2)),
            dma((2, n, heads)), dma((n, heads)),
            dma((n, 3)), dma((n, 2)),
            dma((heads, n, 2)), dma((n, heads)),
            dma((n, heads)), dma((n + 1, heads)),
            dma((n,)), dma((n,)),
        ],
        compiler_params=pltpu.CompilerParams(
            collective_id=0, has_side_effects=True, vmem_limit_bytes=VMEM_BYTES
        ),
        cost_estimate=pl.CostEstimate(
            flops=14 * rows * rows * n * width + 2 * rows * width * feats * nh,
            bytes_accessed=16 * rows * width,
            transcendentals=2 * rows * rows * n * heads,
        ),
    )(key_list[0], key_count, query_states[0], key_states[0], value_states[0], output_grad[0], w_out)
    dq, dk, dv, grad_features = pl.pallas_call(
        finish_kernel,
        out_shape=[block, block, block, jax.ShapeDtypeStruct((3, 1, heads), F32)],
        in_specs=[vmem] * 4,
        out_specs=[vmem] * 4,
    )(dq, dk, dv, feat)
    return dq[None], dk[None], dv[None], jnp.transpose(grad_features, (1, 2, 0))


def solution(mesh):
    in_specs = (
        P(("grp", "clip"), "seq", "head"),
        P(("grp", "clip"), "seq", "head"),
        P(("grp", "clip"), "seq", "head"),
        P(("grp", "clip"), "seq", "head"),
        P("head", None),
        P(("grp", "clip"), None, None),
        P(("grp", "clip"), None),
    )
    out_specs = (
        P(("grp", "clip"), "seq", "head"),
        P(("grp", "clip"), "seq", "head"),
        P(("grp", "clip"), "seq", "head"),
        P(("grp", "clip"), "head", None),
    )
    return jax.shard_map(
        per_device, mesh=mesh, in_specs=in_specs, out_specs=out_specs, check_vma=False
    )
```

```python
import functools
import math

import jax
import jax.numpy as jnp
from jax import lax
from jax.experimental import pallas as pl
from jax.experimental.pallas import tpu as pltpu
from jax.sharding import PartitionSpec as P

HD = 128
TILE = 256


def attend(query_tiles, key_buf, value_buf, grad_tiles, buf_slots, counts):
    score_scale = HD ** (-0.5)
    tile_count, tile_rows, feat_width = query_tiles.shape
    slot_count = buf_slots.shape[1]
    key_span = slot_count * tile_rows
    buf_tiles = key_buf.shape[0]
    key_sel = key_buf[buf_slots].reshape(tile_count, key_span, feat_width)
    value_sel = value_buf[buf_slots].reshape(tile_count, key_span, feat_width)
    allowed = jnp.arange(key_span)[None, :] // tile_rows < counts[:, None]

    def head_step(head_idx, carried):
        query_acc, key_acc, value_acc = carried
        col_start = head_idx * HD
        query_head = lax.dynamic_slice_in_dim(query_tiles, col_start, HD, 2)
        key_head = lax.dynamic_slice_in_dim(key_sel, col_start, HD, 2)
        value_head = lax.dynamic_slice_in_dim(value_sel, col_start, HD, 2)
        grad_head = lax.dynamic_slice_in_dim(grad_tiles, col_start, HD, 2)
        scores = (
            jnp.einsum("iqe,ike->iqk", query_head, key_head, preferred_element_type=jnp.float32)
            * score_scale
        )
        scores = jnp.where(allowed[:, None, :], scores, -jnp.inf)
        row_max = jnp.max(scores, axis=-1, keepdims=True)
        log_norm = row_max + jnp.log(jnp.sum(jnp.exp(scores - row_max), axis=-1, keepdims=True))
        weights = jnp.exp(scores - log_norm)
        weights_b = weights.astype(jnp.bfloat16)
        attn_out = jnp.einsum(
            "iqk,ike->iqe", weights_b, value_head, preferred_element_type=jnp.float32
        ).astype(jnp.bfloat16)
        row_delta = jnp.sum(
            grad_head.astype(jnp.float32) * attn_out.astype(jnp.float32), axis=-1, keepdims=True
        )
        dprob = jnp.einsum(
            "iqe,ike->iqk", grad_head, value_head, preferred_element_type=jnp.float32
        )
        dscore = (weights * (dprob - row_delta)).astype(jnp.bfloat16)
        query_head_grad = score_scale * jnp.einsum(
            "iqk,ike->iqe", dscore, key_head, preferred_element_type=jnp.float32
        )
        key_head_grad = score_scale * jnp.einsum(
            "iqk,iqe->ike", dscore, query_head, preferred_element_type=jnp.float32
        )
        value_head_grad = jnp.einsum(
            "iqk,iqe->ike", weights_b, grad_head, preferred_element_type=jnp.float32
        )
        query_acc = lax.dynamic_update_slice_in_dim(query_acc, query_head_grad, col_start, 2)
        key_acc = lax.dynamic_update_slice_in_dim(key_acc, key_head_grad, col_start, 2)
        value_acc = lax.dynamic_update_slice_in_dim(value_acc, value_head_grad, col_start, 2)
        return (query_acc, key_acc, value_acc)

    start_state = (
        jnp.zeros((tile_count, tile_rows, feat_width), jnp.float32),
        jnp.zeros((tile_count, key_span, feat_width), jnp.float32),
        jnp.zeros((tile_count, key_span, feat_width), jnp.float32),
    )
    query_full, key_sel_grad, value_sel_grad = lax.fori_loop(
        0, feat_width // HD, head_step, start_state
    )
    live_slot = jnp.arange(slot_count)[None, :] < counts[:, None]
    routing = (
        (buf_slots[:, :, None] == jnp.arange(buf_tiles)[None, None, :]) & live_slot[:, :, None]
    ).astype(jnp.float32)
    key_grad_buf = jnp.einsum(
        "imb,imr->br",
        routing,
        key_sel_grad.reshape(tile_count, slot_count, tile_rows * feat_width),
        precision=lax.Precision.HIGHEST,
    )
    value_grad_buf = jnp.einsum(
        "imb,imr->br",
        routing,
        value_sel_grad.reshape(tile_count, slot_count, tile_rows * feat_width),
        precision=lax.Precision.HIGHEST,
    )
    return (
        query_full,
        key_grad_buf.reshape(buf_tiles, tile_rows, feat_width),
        value_grad_buf.reshape(buf_tiles, tile_rows, feat_width),
    )


def head_squares(grads_full, head_count):
    rows = grads_full.reshape(-1, head_count, HD)
    return jnp.sum(rows * rows, axis=(0, 2))


def gathered_plan(query_states, key_states, value_states, output_grad, w_out, key_list, key_count):
    seq_count = lax.axis_size("seq")
    seq_index = lax.axis_index("seq")
    tok_rows = query_states.shape[1]
    feat_width = query_states.shape[2]
    head_count = feat_width // HD
    tile_count = tok_rows // TILE
    first_tile = seq_index * tile_count
    own_lists = lax.dynamic_slice_in_dim(key_list[0], first_tile, tile_count, 0)
    own_counts = lax.dynamic_slice_in_dim(key_count[0], first_tile, tile_count, 0)
    grad_out = lax.dot_general(
        lax.all_gather(output_grad, "head", axis=2, tiled=True)[0],
        w_out,
        (((1,), (1,)), ((), ())),
        preferred_element_type=jnp.float32,
    ).astype(jnp.bfloat16)
    query_tiles = query_states[0].reshape(tile_count, TILE, feat_width)
    grad_tiles = grad_out.reshape(tile_count, TILE, feat_width)
    key_whole, value_whole = (
        lax.all_gather(key_states, "seq", axis=1, tiled=True),
        lax.all_gather(value_states, "seq", axis=1, tiled=True),
    )
    key_buf = key_whole[0].reshape(-1, TILE, feat_width)
    value_buf = value_whole[0].reshape(-1, TILE, feat_width)
    query_full, key_grad_buf, value_grad_buf = attend(
        query_tiles, key_buf, value_buf, grad_tiles, own_lists, own_counts
    )
    buf_rows = key_grad_buf.shape[0] * TILE
    key_sum, value_sum = (
        lax.psum_scatter(
            key_grad_buf.reshape(1, buf_rows, feat_width).astype(jnp.bfloat16),
            "seq",
            scatter_dimension=1,
            tiled=True,
        ).astype(jnp.float32),
        lax.psum_scatter(
            value_grad_buf.reshape(1, buf_rows, feat_width).astype(jnp.bfloat16),
            "seq",
            scatter_dimension=1,
            tiled=True,
        ).astype(jnp.float32),
    )
    key_full = key_sum[0]
    value_full = value_sum[0]
    query_rows = query_full.reshape(tok_rows, feat_width)
    local_sums = jnp.stack(
        [
            head_squares(query_rows, head_count),
            head_squares(key_full, head_count),
            head_squares(value_full, head_count),
        ],
        axis=-1,
    )
    total_sums = lax.psum(local_sums, "seq")
    grad_features = jnp.log(total_sums / (seq_count * tok_rows * HD) + 1e-06)
    return (
        query_rows.astype(jnp.bfloat16)[None],
        key_full.astype(jnp.bfloat16)[None],
        value_full.astype(jnp.bfloat16)[None],
        grad_features[None],
    )


MESH_ID = pl.DeviceIdType.MESH
VMEM_BYTES = 58 * 1024 * 1024
NEG_BIG = -1e30
OG_CUTS = 2
AHEAD = 1
F32 = jnp.float32
BF16 = jnp.bfloat16


def dot_nt(a, b):
    return lax.dot_general(a, b, (((1,), (1,)), ((), ())), preferred_element_type=F32)


def dot_nn(a, b):
    return lax.dot_general(a, b, (((1,), (0,)), ((), ())), preferred_element_type=F32)


def fused_kernel(
    n, nh, gc, list_ref, count_ref, q_ref, k_hbm, v_hbm, og_ref, w_hbm,
    dq_ref, dk_ref, dv_ref, feat_ref,
    k_ref, v_ref, w_ref, bias_ref, q_all, g_all, og_all, g_acc, probs, top_ref, inv_ref,
    lse_all, eps_all, part, chain, kt_ref, acc_k, acc_v, acc_q, sq_all,
    guest_out, guest_in, guest_send, guest_recv, back_send, back_recv, load_sem, og_send, og_recv, q_send, q_recv, g_send, g_recv, lse_send, lse_recv,
    eps_send, eps_recv, chain_send, chain_recv, sq_send, sq_recv,
):
    z = lax.axis_index("seq")
    hx = lax.axis_index("head")
    rows, width = q_ref.shape
    heads = width // HD
    feats = og_ref.shape[1]
    key_tiles = rows // TILE
    scale = HD ** (-0.5)
    scale2 = scale * math.log2(math.e)
    has_left = z > 0
    has_right = z < n - 1
    gw = gc * HD
    is_end = (z == 0) | (z == n - 1)
    host_low, host_high = z == 1, z == n - 2
    is_host = (host_low | host_high) if gc else z < 0
    guest = jnp.where(host_low, 0, n - 1)
    host_of = jnp.where(z == 0, 1, n - 2)

    def inner(d):
        return (d > 0) & (d < n - 1)

    def may_go(way, guest_part):
        to = z + (1 - 2 * way)
        return inner(to) if guest_part else (to >= 0) & (to < n)

    loads = [
        pltpu.make_async_copy(src, dst, load_sem.at[i])
        for i, (src, dst) in enumerate(
            ((q_ref, q_all.at[z]), (og_ref, og_all.at[hx]), (w_hbm, w_ref), (k_hbm, k_ref.at[:, 0:width]), (v_hbm, v_ref.at[:, 0:width]))
        )
    ]
    for load in loads:
        load.start()

    def remote(src, dst, ssem, rsem, axis, idx):
        return pltpu.make_async_remote_copy(
            src_ref=src, dst_ref=dst, send_sem=ssem, recv_sem=rsem,
            device_id={axis: idx}, device_id_type=MESH_ID,
        )

    def cols(h):
        return pl.ds(pl.multiple_of(h * HD, HD), HD)

    barrier = pltpu.get_barrier_semaphore()
    for i in range(1, n):
        pl.semaphore_signal(barrier, inc=1, device_id={"seq": lax.rem(z + i, n)}, device_id_type=MESH_ID)
    for i in range(1, nh):
        pl.semaphore_signal(barrier, inc=1, device_id={"head": lax.rem(hx + i, nh)}, device_id_type=MESH_ID)
    pl.semaphore_wait(barrier, n - 1 + nh - 1)

    def og_rows(c):
        return pl.ds(c * (rows // OG_CUTS), rows // OG_CUTS)

    def og_copy(i, c):
        return remote(og_ref.at[og_rows(c)], og_all.at[hx, og_rows(c)], og_send.at[i, c], og_recv.at[hx, c], "head", lax.rem(hx + i, nh))

    def og_arrival(j, c):
        ref = og_all.at[j, og_rows(c)]
        return remote(ref, ref, og_send.at[0, c], og_recv.at[j, c], "head", hx)

    q_parts = [(0, gw), (gw, width - gw)] if gc else [(0, width)]

    def q_own(way, p):
        at = pl.ds(*q_parts[p])
        return remote(q_ref.at[:, at], q_all.at[z, :, at], q_send.at[way, z, p], q_recv.at[z, p], "seq", z + (1 - 2 * way))

    def q_copy(b, way, p):
        ref = q_all.at[b, :, pl.ds(*q_parts[p])]
        return remote(ref, ref, q_send.at[way, b, p], q_recv.at[b, p], "seq", z + (1 - 2 * way))

    def lend(i):
        src, dst = ((k_hbm, k_ref), (v_hbm, v_ref))[i]
        return remote(src.at[:, 0:gw], dst.at[:, width : width + gw], guest_send.at[i], guest_recv.at[i], "seq", host_of)

    def lent(i):
        ref = (k_ref, v_ref)[i].at[:, width : width + gw]
        return remote(ref, ref, guest_send.at[i], guest_recv.at[i], "seq", z)

    def back_copy(h):
        return remote(guest_out.at[h], guest_in.at[h], back_send.at[h], back_recv.at[h], "seq", guest)

    def back_arrival(h):
        return remote(guest_in.at[h], guest_in.at[h], back_send.at[h], back_recv.at[h], "seq", z)

    def g_copy(b, h, way):
        return remote(g_all.at[b, h], g_all.at[b, h], g_send.at[way, b, h], g_recv.at[b, h], "seq", z + (1 - 2 * way))

    def g_own(h, way, c):
        ref = g_all.at[z, h, og_rows(c)]
        return remote(ref, ref, g_send.at[way, z, h], g_recv.at[z, h], "seq", z + (1 - 2 * way))

    def lse_ref(d, p):
        return lse_all.at[d, 0:gc] if p else lse_all.at[d, gc:heads]

    def lse_copy(d, i, p, k):
        return remote(lse_ref(d, p), lse_ref(d, p), lse_send.at[i, k], lse_recv.at[d, p], "seq", lax.rem(z + i, n))

    def lse_arrival(d, p):
        return remote(lse_ref(d, p), lse_ref(d, p), lse_send.at[0, 0], lse_recv.at[d, p], "seq", z)

    def eps_copy(d, h, i, k):
        return remote(eps_all.at[d, h], eps_all.at[d, h], eps_send.at[h, i, k], eps_recv.at[d, h], "seq", lax.rem(z + i, n))

    def eps_arrival(d, h):
        return remote(eps_all.at[d, h], eps_all.at[d, h], eps_send.at[h, 0, 0], eps_recv.at[d, h], "seq", z)

    def lse_sends(act):
        for i in range(1, n):
            act(lse_copy(z, i, 0, 0))
            if gc:
                @pl.when(inner(z) & inner(lax.rem(z + i, n)))
                def _():
                    act(lse_copy(z, i, 1, 1))

                    @pl.when(is_host)
                    def _():
                        act(lse_copy(guest, i, 1, 2))

    def eps_sends(h, act):
        for i in range(1, n):
            @pl.when((h >= gc) | (inner(z) & inner(lax.rem(z + i, n))))
            def _():
                act(eps_copy(z, h, i, 0))

            @pl.when((h < gc) & is_host & inner(lax.rem(z + i, n)))
            def _():
                act(eps_copy(guest, h, i, 1))

    def chain_copy(b, h, way):
        slot = b if way == 0 else jnp.where(b == z - 1, n, b)
        return remote(part.at[b, h], chain.at[slot, h], chain_send.at[b, h], chain_recv.at[slot, h], "seq", z + (1 - 2 * way))

    def chain_arrival(slot, h):
        return remote(chain.at[slot, h], chain.at[slot, h], chain_send.at[0, h], chain_recv.at[slot, h], "seq", z)

    def sq_copy(i):
        return remote(sq_all.at[z], sq_all.at[z], sq_send.at[i], sq_recv.at[z], "seq", lax.rem(z + i, n))

    def sq_arrival(d):
        return remote(sq_all.at[d], sq_all.at[d], sq_send.at[0], sq_recv.at[d], "seq", z)

    def q_own_all(act):
        for p in range(len(q_parts)):
            for way in range(2):
                @pl.when(may_go(way, gc > 0 and p == 0))
                def _():
                    act(q_own(way, p))

    def q_on(s, act):
        for way, b in ((0, z - s), (1, z + s)):
            for p in range(len(q_parts)):
                @pl.when((b >= 0) & (b < n) & may_go(way, gc > 0 and p == 0))
                def _():
                    act(q_copy(b, way, p))

    def g_own_starts(h, c):
        for way in range(2):
            @pl.when(may_go(way, False) & ((h >= gc) | may_go(way, True)))
            def _():
                g_own(h, way, c).start()

    def g_sends(b, h, way, act):
        @pl.when((b >= 0) & (b < n) & may_go(way, False) & ((h >= gc) | may_go(way, True)))
        def _():
            act(g_copy(b, h, way))

    for i in range(1, nh):
        for c in range(OG_CUTS):
            og_copy(i, c).start()
    q_own_all(lambda c: c.start())
    if gc:
        @pl.when(is_end)
        def _():
            lend(0).start()
            lend(1).start()

    tiles, slots = list_ref.shape
    for i in range(tiles):
        for j in range(key_tiles):
            at = (i % key_tiles) * TILE
            for k, owner in enumerate((z, guest) if gc else (z,)):
                bias = jnp.float32(NEG_BIG)
                for m in range(slots):
                    hit = (list_ref[i, m] == owner * key_tiles + j) & (m < count_ref[0, i])
                    bias = jnp.where(hit, jnp.float32(0.0), bias)
                bias_ref[k, i // key_tiles, j, :, at : at + TILE] = jnp.full((1, TILE), bias, F32)

    wide = 256 if width % 256 == 0 else HD

    def features_of(block, j, part_rows, add):
        span = pl.ds(pl.multiple_of(j * feats, HD), feats)

        @pl.loop(0, width // wide)
        def _(c):
            at = pl.ds(pl.multiple_of(c * wide, wide), wide)
            term = dot_nt(block[part_rows, :], w_ref[at, span])
            if add:
                g_acc[c, part_rows, :] = g_acc[c, part_rows, :] + term
            else:
                g_acc[c, part_rows, :] = term

    for load in loads:
        load.wait()
    features_of(og_all.at[hx], hx, slice(0, rows), False)

    def gradient_rows(c):
        part_rows = og_rows(c)
        for i in range(1, nh):
            j = lax.rem(hx + i, nh)
            og_arrival(j, c).wait_recv()
            features_of(og_all.at[j], j, part_rows, True)
        for h in range(heads):
            lo = h * HD
            g_all[z, h, part_rows, :] = g_acc[lo // wide, part_rows, lo % wide : lo % wide + HD].astype(BF16)
            g_own_starts(h, c)

    def q_hop(s):
        for way, b in ((0, z - s), (1, z + s)):
            @pl.when((b >= 0) & (b < n))
            def _():
                for p in range(len(q_parts)):
                    @pl.when(inner(z) if gc > 0 and p == 0 else z >= 0)
                    def _():
                        q_copy(b, way, p).wait_recv()

                        @pl.when(may_go(way, gc > 0 and p == 0))
                        def _():
                            q_copy(b, way, p).start()

    first_head = jnp.where(is_end, gc, 0)

    def softmax_rows(b, low, high):
        @pl.loop(low, high)
        def _(v):
            mine = v < heads
            h = jnp.where(mine, v, v - heads)
            ts = []
            for j in range(key_tiles):
                t = dot_nt(k_ref[j * TILE : (j + 1) * TILE, cols(v)], q_all[b, :, cols(h)])
                ts.append(t * scale2 + bias_ref[jnp.where(mine, 0, 1), b, j])
            top = functools.reduce(jnp.maximum, [jnp.max(t, axis=0, keepdims=True) for t in ts])
            total = jnp.zeros((1, rows), F32)
            for j in range(key_tiles):
                p = jnp.exp2(ts[j] - top)
                total += jnp.sum(p, axis=0, keepdims=True)
                probs[b, v, j * TILE : (j + 1) * TILE, :] = p.astype(BF16)
            top_ref[v, b] = top
            inv_ref[v, b] = 1.0 / total
            lse_all[jnp.where(mine, z, guest), h, b] = top + jnp.log2(total)

    def softmax_at(s):
        @pl.when(z - s >= 0)
        def _():
            softmax_rows(z - s, first_head, heads)

        @pl.when(z + s < n)
        def _():
            softmax_rows(z + s, first_head, heads)

    @pl.loop(0, heads)
    def _(h):
        kt_ref[h] = jnp.transpose(k_ref[:, cols(h)].astype(F32)).astype(BF16)

    softmax_rows(z, first_head, heads)
    for s in range(1, max(n, OG_CUTS + 1)):
        if s < n:
            q_hop(s)
        if s <= OG_CUTS:
            gradient_rows(s - 1)
        if s < n:
            softmax_at(s)
    def g_hop(s, h):
        for way, b in ((0, z - s), (1, z + s)):
            @pl.when((h >= 0) & (h < heads) & (b >= 0) & (b < n) & ((h >= gc) | inner(z)))
            def _():
                g_copy(b, h, way).wait_recv()
                if s < n - 1:
                    g_sends(b, h, way, lambda c: c.start())

    def g_hops(t):
        for s in range(1, n):
            g_hop(s, t + (n - 1 - s) + AHEAD)

    lead = n - 2 + AHEAD

    @pl.loop(0, lead)
    def _(step):
        g_hops(step - lead)

    if gc:
        @pl.when(is_host)
        def _():
            lent(0).wait_recv()
            lent(1).wait_recv()

            @pl.loop(heads, heads + gc)
            def _(v):
                kt_ref[v] = jnp.transpose(k_ref[:, cols(v)].astype(F32)).astype(BF16)

            @pl.loop(0, n)
            def _(b):
                softmax_rows(b, heads, heads + gc)

    lse_sends(lambda c: c.start())

    def dprobs(b, v, h, j):
        return dot_nt(v_ref[j * TILE : (j + 1) * TILE, cols(v)], g_all[b, h])

    def holders(h):
        return jnp.where(h < gc, jnp.where(is_end, 0, jnp.where(is_host, 2, 1)), 1)

    def first_pass(h):
        @pl.loop(0, holders(h))
        def _(k):
            v = h + k * heads
            owner = jnp.where(k == 0, z, guest)

            @pl.loop(0, n)
            def _(b):
                eps = jnp.zeros((1, rows), F32)
                for j in range(key_tiles):
                    p = probs[b, v, j * TILE : (j + 1) * TILE, :].astype(F32)
                    eps += jnp.sum(p * dprobs(b, v, h, j), axis=0, keepdims=True)
                eps_all[owner, h, b] = eps * inv_ref[v, b]

        eps_sends(h, lambda c: c.start())

    def second_pass(h):
        for i in range(1, n):
            d = lax.rem(z + i, n)
            skip = (d == guest) & is_host

            @pl.when((h >= gc) | (inner(z) & jnp.logical_not(skip)))
            def _():
                eps_arrival(d, h).wait_recv()

        for b in range(n):
            part[b, h] = jnp.zeros((HD, rows), BF16)

        @pl.loop(0, holders(h))
        def _(k):
            v = h + k * heads
            acc_k[...] = jnp.zeros_like(acc_k)
            acc_v[...] = jnp.zeros_like(acc_v)

            @pl.loop(0, n)
            def _(b):
                logs = [lse_all[d, h, b] for d in range(n)]
                top = functools.reduce(jnp.maximum, logs)
                log_norm = top + jnp.log2(sum(jnp.exp2(x - top) for x in logs))
                delta = sum(jnp.exp2(logs[d] - log_norm) * eps_all[d, h, b] for d in range(n))
                share = jnp.exp2(top_ref[v, b] - log_norm)
                q_b = q_all[b, :, cols(h)]
                g_b = g_all[b, h]
                dq_t = jnp.zeros((HD, rows), F32)
                for j in range(key_tiles):
                    at = slice(j * TILE, (j + 1) * TILE)
                    p = probs[b, v, at, :].astype(F32) * share
                    ds = (p * (dprobs(b, v, h, j) - delta)).astype(BF16)
                    acc_v[at, :] += dot_nn(p.astype(BF16), g_b)
                    acc_k[at, :] += dot_nn(ds, q_b)
                    dq_t += dot_nn(kt_ref[v, :, at], ds)
                part[b, h] = (part[b, h].astype(F32) + dq_t * scale).astype(BF16)

            key_full = acc_k[...] * scale
            value_full = acc_v[...]

            @pl.when(k == 0)
            def _():
                dk_ref[:, cols(h)] = key_full.astype(BF16)
                dv_ref[:, cols(h)] = value_full.astype(BF16)
                sq_all[z, 1, h] = jnp.sum(key_full * key_full, axis=0, keepdims=True)
                sq_all[z, 2, h] = jnp.sum(value_full * value_full, axis=0, keepdims=True)

            if gc:
                @pl.when(k == 1)
                def _():
                    guest_out[h, 0] = key_full.astype(BF16)
                    guest_out[h, 1] = value_full.astype(BF16)
                    back_copy(h).start()

    def take_back(h):
        @pl.when((h >= 0) & (h < gc) & is_end)
        def _():
            back_arrival(h).wait_recv()
            for i, ref in enumerate((dk_ref, dv_ref)):
                ref[:, cols(h)] = guest_in[h, i]
                full = guest_in[h, i].astype(F32)
                sq_all[z, i + 1, h] = jnp.sum(full * full, axis=0, keepdims=True)

    def comes(h, way):
        far = z if way == 0 else n - 1 - z
        return far > jnp.where(h < gc, 1, 0)

    def chain_sends(h, way, act):
        for i in reversed(range(1, n)):
            b = z + i if way == 0 else z - i

            @pl.when((b >= 0) & (b < n) & ((h >= gc) | inner(z)))
            def _():
                act(b)

    def chain_hop(h, way):
        def hop(b):
            @pl.when(comes(h, way))
            def _():
                chain_arrival(b, h).wait_recv()
                part[b, h] = (part[b, h].astype(F32) + chain[b, h].astype(F32)).astype(BF16)

            chain_copy(b, h, way).start()

        @pl.when((h >= 0) & (h < heads))
        def _():
            chain_sends(h, way, hop)

    def chain_hops(t, starts):
        for way, far in ((0, z), (1, n - 1 - z)):
            @pl.when((far == 0) if starts else (far > 0))
            def _():
                chain_hop(t - 1 - far, way)

    def own_sum(h):
        @pl.when((h >= 0) & (h < heads))
        def _():
            acc_q[...] = jnp.zeros_like(acc_q)

            @pl.when((h >= gc) | inner(z))
            def _():
                acc_q[...] = part[z, h].astype(F32)

            for way, slot in ((0, z), (1, n)):
                @pl.when(comes(h, way))
                def _():
                    chain_arrival(slot, h).wait_recv()
                    acc_q[...] += chain[slot, h].astype(F32)

            query_full = jnp.transpose(acc_q[...])
            dq_ref[:, cols(h)] = query_full.astype(BF16)
            sq_all[z, 0, h] = jnp.sum(query_full * query_full, axis=0, keepdims=True)

    @pl.loop(0, heads + n)
    def _(t):
        g_hops(t)

        @pl.when((t >= 0) & (t < heads))
        def _():
            first_pass(t)

        chain_hops(t, False)

        @pl.when(t == 1)
        def _():
            for i in range(1, n):
                d = lax.rem(z + i, n)
                lse_arrival(d, 0).wait_recv()
                if gc:
                    skip = (d == guest) & is_host

                    @pl.when(inner(z) & jnp.logical_not(skip))
                    def _():
                        lse_arrival(d, 1).wait_recv()

        @pl.when((t >= 1) & (t <= heads))
        def _():
            second_pass(t - 1)

        chain_hops(t, True)
        own_sum(t - 1 - jnp.maximum(z, n - 1 - z))
        if gc:
            take_back(t - 3)

    for i in range(1, n):
        sq_copy(i).start()
    for i in range(1, n):
        sq_arrival(lax.rem(z + i, n)).wait_recv()
    total = functools.reduce(jnp.add, [sq_all[d] for d in range(n)])
    mean = jnp.sum(total, axis=-1, keepdims=True) / (n * rows * HD)
    logs = jnp.log(mean + 1e-06)
    lane = lax.broadcasted_iota(jnp.int32, (1, HD), 1)
    for j in range(3):
        feat_ref[j] = sum(jnp.where(lane == h, logs[j, h], 0.0) for h in range(heads))

    for i in range(1, nh):
        for c in range(OG_CUTS):
            og_copy(i, c).wait_send()
    for i in range(1, n):
        sq_copy(i).wait_send()
    lse_sends(lambda c: c.wait_send())
    q_own_all(lambda c: c.wait_send())
    for s in range(1, n - 1):
        q_on(s, lambda c: c.wait_send())
    if gc:
        @pl.when(is_end)
        def _():
            lend(0).wait_send()
            lend(1).wait_send()

    @pl.loop(0, heads)
    def _(h):
        for way in range(2):
            for s in range(n - 1):
                b = z - s if way == 0 else z + s

                @pl.when((h >= gc) | inner(z) | (b == z))
                def _():
                    g_sends(b, h, way, lambda c: c.wait_send())

            chain_sends(h, way, lambda b: chain_copy(b, h, way).wait_send())
        eps_sends(h, lambda c: c.wait_send())
        if gc:
            @pl.when((h < gc) & is_host)
            def _():
                back_copy(h).wait_send()


def finish_kernel(dq_in, dk_in, dv_in, feat_in, dq_ref, dk_ref, dv_ref, feat_ref):
    dq_ref[...] = dq_in[...]
    dk_ref[...] = dk_in[...]
    dv_ref[...] = dv_in[...]
    feat_ref[...] = feat_in[:, :, : feat_ref.shape[2]]


def fused_bytes(n, nh, rows, width, feats):
    block = rows * width * 2
    kept = n * (width // HD) * rows * rows * 3
    return block * (5 + 3 * n + n + 1) + rows * feats * 2 * nh + width * feats * nh * 2 + 2 * block + kept


def per_device(query_states, key_states, value_states, output_grad, w_out, key_list, key_count):
    n = lax.axis_size("seq")
    nh = lax.axis_size("head")
    rows, width = query_states.shape[1:]
    feats = output_grad.shape[2]
    if n < 2 or fused_bytes(n, nh, rows, width, feats) > VMEM_BYTES * 3 // 4:
        return gathered_plan(
            query_states, key_states, value_states, output_grad, w_out, key_list, key_count
        )
    heads = width // HD
    key_tiles = rows // TILE
    wide = 256 if width % 256 == 0 else HD
    gc = heads // 3 if n >= 4 else 0
    gn = max(gc, 1)
    vmem = pl.BlockSpec(memory_space=pltpu.VMEM)
    dma = pltpu.SemaphoreType.DMA
    block = jax.ShapeDtypeStruct((rows, width), BF16)
    dq, dk, dv, feat = pl.pallas_call(
        functools.partial(fused_kernel, n, nh, gc),
        out_shape=[block, block, block, jax.ShapeDtypeStruct((3, 1, HD), F32)],
        in_specs=[pl.BlockSpec(memory_space=pltpu.SMEM)] * 2 + [pl.BlockSpec(memory_space=pl.ANY)] * 5,
        out_specs=[vmem] * 4,
        scratch_shapes=[
            pltpu.VMEM((rows, width + gc * HD), BF16),
            pltpu.VMEM((rows, width + gc * HD), BF16),
            pltpu.VMEM((width, feats * nh), BF16),
            pltpu.VMEM((2, n, key_tiles, 1, rows), F32),
            pltpu.VMEM((n, rows, width), BF16),
            pltpu.VMEM((n, heads, rows, HD), BF16),
            pltpu.VMEM((nh, rows, feats), BF16),
            pltpu.VMEM((width // wide, rows, wide), F32),
            pltpu.VMEM((n, heads + gc, rows, rows), BF16),
            pltpu.VMEM((heads + gc, n, 1, rows), F32),
            pltpu.VMEM((heads + gc, n, 1, rows), F32),
            pltpu.VMEM((n, heads, n, 1, rows), F32),
            pltpu.VMEM((n, heads, n, 1, rows), F32),
            pltpu.VMEM((n, heads, HD, rows), BF16),
            pltpu.VMEM((n + 1, heads, HD, rows), BF16),
            pltpu.VMEM((heads + gc, HD, rows), BF16),
            pltpu.VMEM((rows, HD), F32),
            pltpu.VMEM((rows, HD), F32),
            pltpu.VMEM((HD, rows), F32),
            pltpu.VMEM((n, 3, heads, 1, HD), F32),
            pltpu.VMEM((gn, 2, rows, HD), BF16),
            pltpu.VMEM((gn, 2, rows, HD), BF16),
            dma((2,)), dma((2,)), dma((gn,)), dma((gn,)),
            dma((5,)),
            dma((nh, OG_CUTS)), dma((nh, OG_CUTS)),
            dma((2, n, 2)), dma((n, 2)),
            dma((2, n, heads)), dma((n, heads)),
            dma((n, 3)), dma((n, 2)),
            dma((heads, n, 2)), dma((n, heads)),
            dma((n, heads)), dma((n + 1, heads)),
            dma((n,)), dma((n,)),
        ],
        compiler_params=pltpu.CompilerParams(
            collective_id=0, has_side_effects=True, vmem_limit_bytes=VMEM_BYTES
        ),
        cost_estimate=pl.CostEstimate(
            flops=14 * rows * rows * n * width + 2 * rows * width * feats * nh,
            bytes_accessed=16 * rows * width,
            transcendentals=2 * rows * rows * n * heads,
        ),
    )(key_list[0], key_count, query_states[0], key_states[0], value_states[0], output_grad[0], w_out)
    dq, dk, dv, grad_features = pl.pallas_call(
        finish_kernel,
        out_shape=[block, block, block, jax.ShapeDtypeStruct((3, 1, heads), F32)],
        in_specs=[vmem] * 4,
        out_specs=[vmem] * 4,
    )(dq, dk, dv, feat)
    return dq[None], dk[None], dv[None], jnp.transpose(grad_features, (1, 2, 0))


def solution(mesh):
    in_specs = (
        P(("grp", "clip"), "seq", "head"),
        P(("grp", "clip"), "seq", "head"),
        P(("grp", "clip"), "seq", "head"),
        P(("grp", "clip"), "seq", "head"),
        P("head", None),
        P(("grp", "clip"), None, None),
        P(("grp", "clip"), None),
    )
    out_specs = (
        P(("grp", "clip"), "seq", "head"),
        P(("grp", "clip"), "seq", "head"),
        P(("grp", "clip"), "seq", "head"),
        P(("grp", "clip"), "head", None),
    )
    return jax.shard_map(
        per_device, mesh=mesh, in_specs=in_specs, out_specs=out_specs, check_vma=False
    )
```
